128 devices in a mesh: dp: 2 (over core), member: 4 (over x), space: 16 (over y, z).
Axes of the slice: x: 4, y: 4, z: 4, core: 2. Of those that a mesh axis runs over, the one named last changes fastest.
Arguments:
- latents: bfloat16 [2, 8, 32768, 512], P('dp', 'member', 'space'), may hold values from -6 to 6
- edge_weight: bfloat16 [128, 4, 128, 128], P('space'), may hold values from -0.25 to 0.25
- block_ids: int32 [128, 4], P('space'), may hold values from 0 to 19, as said below
- block_count: int32 [128], P('space'), may hold values from 1 to 4, as said below
- w_in: bfloat16 [512, 512], replicated, may hold values from -0.25 to 0.25
- w_out: bfloat16 [83, 512], replicated, may hold values from -0.25 to 0.25
- targets: bfloat16 [2, 83, 16384], P('dp', None, 'space'), may hold values from -6 to 6
- area: float32 [16384], P('space'), may hold values from 0.2 to 2
- var_weight: float32 [83], replicated, may hold values from 0.2 to 2
Outputs:
- grad_latent: float32 [2, 8, 32768, 512], P('dp', 'member', 'space')
- grad_w_in: float32 [512, 512], P(('dp', 'member', 'space'))
- grad_w_out: float32 [83, 512], P(None, ('dp', 'member', 'space'))
The draws below stay inside these ranges and needn't reach their ends.
Inputs may be any that keep to these rules, and one draw needn't show every extreme that they name: Slots k >= block_count[t] of a tile are padding; some tile has 4 live slots. `block_ids`: block numbers are counted in the tile's own space index's blocks extended by 2 blocks on each side. On every space index, the first slot of its first tile reads a block below its own and the first slot of its last tile a block above its own.
All inputs are finite; a program needn't handle non-finite values.
Results may differ from the reference program's by a relative error of at most 0.02.
Values may be sent and summed in bfloat16 or wider, within the bound.
No kernel may reach another device: no remote copies, remote signals or barrier semaphores. Data moves between devices by JAX's collectives and lax.ppermute only.
A program may use at most 128 MiB of HBM per device.

```python
import math
import jax
import jax.numpy as jnp
from jax import lax

C = 512
HID = 512
V = 83
GT = 128
NB = 128
KMAX = 4
HALO_BLK = 2
NODE_BLK = 16
TILE_DEV = 8
MEMBERS = 8
STATES = 2
TILES = 128
GRID = 16384
NODES = 32768
EXT_BLK = 20


def draw_block_count(key, part):
    key = jax.random.fold_in(key, 11)
    tile_index = jnp.arange(TILES, dtype=jnp.int32)
    pole_distance = jnp.abs(2 * tile_index - (TILES - 1))
    base_count = 1 + 3 * pole_distance * pole_distance // ((TILES - 1) * (TILES - 1))
    jitter = jax.random.randint(key, (TILES,), 0, 2, dtype=jnp.int32)
    return jnp.minimum(base_count + jitter, KMAX).astype(jnp.int32)


def draw_block_ids(key, part):
    key = jax.random.fold_in(key, 23)
    key_all, key_low, key_high = jax.random.split(key, 3)
    uniform_ids = jax.random.randint(key_all, (TILES, KMAX), 0, EXT_BLK, dtype=jnp.int32)
    low_ids = jax.random.randint(key_low, (TILES,), 0, HALO_BLK, dtype=jnp.int32)
    high_ids = EXT_BLK - HALO_BLK + jax.random.randint(key_high, (TILES,), 0, HALO_BLK, dtype=jnp.int32)
    position = jnp.arange(TILES, dtype=jnp.int32) % TILE_DEV
    first_slot = jnp.where(position == 0, low_ids, jnp.where(position == TILE_DEV - 1, high_ids, uniform_ids[:, 0]))
    return uniform_ids.at[:, 0].set(first_slot).astype(jnp.int32)


def block_levels(stream_key, dims, pieces, smallest, high):
    factor_of = 1.0
    for axis_at, blocks in pieces:
        heights = jax.random.uniform(jax.random.fold_in(jax.random.fold_in(stream_key, 6), axis_at), (blocks,), jnp.float32, smallest / len(pieces), high / len(pieces))
        factor_of = factor_of * jnp.repeat(jnp.exp(heights), dims[axis_at] // blocks).reshape((-1,) + (1,) * (len(dims) - 1 - axis_at))
    return factor_of


def bell_draw(key, extent, scale, most, cuts=(), kind=jnp.bfloat16):
    values = scale * jax.random.normal(key, extent, jnp.float32)
    if cuts:
        values = values * block_levels(key, extent, cuts, -0.22, 0.18)
    return jnp.clip(values, -most, most).astype(kind)


def setup_inputs(seed: int = 0) -> dict:
    keys = jax.random.split(jax.random.key(seed), 10)
    latents = bell_draw(keys[0], (STATES, MEMBERS, NODES, C), 1.0, 6.0, ((0, 2), (1, 4), (2, 16)))
    edge_weight = bell_draw(keys[1], (TILES, KMAX, GT, NB), (KMAX * NB) ** -0.5, 0.25, ((0, 16),))
    block_ids = draw_block_ids(jax.random.fold_in(keys[9], 71), 0)
    block_count = draw_block_count(jax.random.fold_in(keys[9], 71), 0)
    w_in = bell_draw(keys[4], (HID, C), C ** -0.5, 0.25)
    w_out = bell_draw(keys[5], (V, HID), HID ** -0.5, 0.25)
    targets = bell_draw(keys[6], (STATES, V, GRID), 1.0, 6.0, ((0, 2), (2, 16)))
    area = jnp.clip(jnp.exp(math.log(2.0) - 2.3025851 * jax.random.uniform(keys[7], (GRID,), jnp.float32) ** block_levels(keys[7], (GRID,), ((0, 16),), -0.2, 0.2)), 0.2, 2.0)
    var_weight = jnp.clip(jnp.exp(jax.random.uniform(keys[8], (V,), jnp.float32, math.log(0.2), math.log(2.0))), 0.2, 2.0)
    return dict(latents=latents, edge_weight=edge_weight, block_ids=block_ids, block_count=block_count, w_in=w_in, w_out=w_out, targets=targets, area=area, var_weight=var_weight)


smooth_width = 0.1

def crps_cotangent(own_fields, all_fields, target_part, cell_weight):
    ensemble_size = all_fields.shape[0]
    to_truth = own_fields - target_part[None]
    truth_term = to_truth / jnp.sqrt(to_truth * to_truth + smooth_width * smooth_width) / ensemble_size

    def add_pair(summed, member_field):
        spread_diff = own_fields - member_field[None]
        return (summed + spread_diff / jnp.sqrt(spread_diff * spread_diff + smooth_width * smooth_width), None)
    spread_sum, _ = lax.scan(add_pair, jnp.zeros_like(own_fields), all_fields)
    result = cell_weight[None] * (truth_term - spread_sum / (ensemble_size * (ensemble_size - 1)))
    return result.astype(jnp.bfloat16)

def padded_blocks(latent):
    blocks = latent.reshape(-1, NB, latent.shape[-1])
    return jnp.pad(blocks, ((HALO_BLK, HALO_BLK), (0, 0), (0, 0)))

def block_anchor():
    return jnp.arange(TILES, dtype=jnp.int32) // TILE_DEV * NODE_BLK

def decode(latent, masked, block_ids):
    padded = padded_blocks(latent)
    anchor = block_anchor()
    summed = jnp.zeros((TILES, GT, latent.shape[-1]), jnp.float32)
    for slot_index in range(KMAX):
        picked = padded[(anchor + block_ids[:, slot_index]).astype(jnp.int32)]
        summed = summed + jnp.einsum('tgj,tjc->tgc', masked[:, slot_index].astype(jnp.float32), picked.astype(jnp.float32))
    return summed.astype(jnp.bfloat16).reshape(GRID, -1)

def reference(latents, edge_weight, block_ids, block_count, w_in, w_out, targets, area, var_weight):
    live_slots = jnp.arange(KMAX, dtype=jnp.int32)[None, :] < block_count[:, None]
    masked = edge_weight * live_slots[:, :, None, None].astype(jnp.bfloat16)
    cell_weight = area[None, :] * var_weight[:, None] / STATES
    cotangents = []
    for state in range(STATES):
        fields = []
        for member in range(MEMBERS):
            grid_latent = decode(latents[state, member], masked, block_ids)
            pre_act = jnp.dot(grid_latent, w_in.T, preferred_element_type=jnp.float32)
            activated = jax.nn.gelu(pre_act).astype(jnp.bfloat16)
            fields.append(jnp.dot(w_out, activated.T, preferred_element_type=jnp.float32).astype(jnp.bfloat16))
        stacked = jnp.stack(fields).astype(jnp.float32)
        cotangents.append(crps_cotangent(stacked, stacked, targets[state].astype(jnp.float32), cell_weight))
    grad_w_in = jnp.zeros((HID, C), jnp.float32)
    grad_w_out = jnp.zeros((V, HID), jnp.float32)
    anchor = block_anchor()
    state_grads = []
    for state in range(STATES):
        member_grads = []
        for member in range(MEMBERS):
            grid_latent = decode(latents[state, member], masked, block_ids)
            pre_act = jnp.dot(grid_latent, w_in.T, preferred_element_type=jnp.float32)
            activated = jax.nn.gelu(pre_act).astype(jnp.bfloat16)
            cotangent = cotangents[state][member]
            grad_act = jnp.dot(cotangent.T, w_out, preferred_element_type=jnp.float32)
            grad_pre = jax.vjp(jax.nn.gelu, pre_act)[1](grad_act)[0].astype(jnp.bfloat16)
            grad_w_out = grad_w_out + jnp.dot(cotangent, activated, preferred_element_type=jnp.float32)
            grad_w_in = grad_w_in + jnp.dot(grad_pre.T, grid_latent, preferred_element_type=jnp.float32)
            grad_grid = jnp.dot(grad_pre, w_in, preferred_element_type=jnp.float32).astype(jnp.bfloat16)
            grad_grid = grad_grid.reshape(TILES, GT, C).astype(jnp.float32)
            padded = jnp.zeros((NODES // NB + 2 * HALO_BLK, NB, C), jnp.float32)
            for slot_index in range(KMAX):
                contrib = jnp.einsum('tgj,tgc->tjc', masked[:, slot_index].astype(jnp.float32), grad_grid)
                padded = padded.at[(anchor + block_ids[:, slot_index]).astype(jnp.int32)].add(contrib)
            member_grads.append(padded[HALO_BLK:HALO_BLK + NODES // NB].reshape(NODES, C))
        state_grads.append(jnp.stack(member_grads))
    return (jnp.stack(state_grads), grad_w_in, grad_w_out)
```

```python
import functools

import jax
import jax.numpy as jnp
from jax import lax
from jax.experimental import pallas as pl
from jax.experimental.pallas import tpu as pltpu
from jax.sharding import PartitionSpec as P

HALO = 2
lat_blocks = 16
smooth_square = 0.1 * 0.1
MIB = 1 << 20
f32 = jnp.float32
bf16 = jnp.bfloat16

NN = (((1,), (0,)), ((), ()))
NT = (((1,), (1,)), ((), ()))


def dot(a, b, dims=NN):
    return lax.dot_general(a, b, dims, preferred_element_type=f32)


def whole(memory_space=pltpu.VMEM):
    return pl.BlockSpec(memory_space=memory_space)


def smem():
    return pl.BlockSpec(memory_space=pltpu.SMEM)


def cost(flops, moved, transcendentals=0):
    return pl.CostEstimate(flops=flops, bytes_accessed=moved, transcendentals=transcendentals)


def params(mib):
    return pltpu.CompilerParams(vmem_limit_bytes=mib * MIB)


def shape(dims, dtype):
    return jax.ShapeDtypeStruct(dims, dtype)


def own_part_kernel(ids, count, lat, weight, w_in, w_out, acc, weight_t, w_in_t, w_out_t):
    members, blocks = lat.shape[0], lat.shape[1]
    tiles, slots = weight.shape[0], weight.shape[1]

    def tile(t, carry):
        parts, at = [], []
        for k in range(slots):
            e = ids[t, k]
            mine = (k < count[t]) & (e >= HALO) & (e < HALO + blocks)
            w = weight[t, k]
            weight_t[t, k] = w.T
            parts.append(jnp.where(mine, w, jnp.zeros_like(w)))
            at.append(jnp.clip(e - HALO, 0, blocks - 1))
        lhs = jnp.concatenate(parts, axis=1)
        for m in range(members):
            rhs = jnp.concatenate([lat[m, a] for a in at], axis=0)
            acc[m, t] = dot(lhs, rhs)
        return carry

    lax.fori_loop(0, tiles, tile, 0)
    w_in_t[...] = w_in[...].T
    w_out_t[...] = w_out[...].T


def gelu_parts(x):
    scale = 0.7978845608028654
    square = x * x
    half = 0.5 + 0.5 * jnp.tanh(x * (scale + (scale * 0.044715) * square))
    return square, half


def fields_kernel(ids, count, acc, low, high, weight, w_in, w_out, lat_out, fields, total):
    t = pl.program_id(0)
    members, slots = acc.shape[0], weight.shape[1]
    total[...] = acc[:, 0]
    for k in range(slots):
        e = ids[t, k]
        live = k < count[t]

        @pl.when(live & (e < HALO))
        def _():
            w = weight[0, k]
            for m in range(members):
                total[m] += dot(w, low[m, e])

        upper = e - (HALO + lat_blocks)

        @pl.when(live & (upper >= 0))
        def _():
            w = weight[0, k]
            for m in range(members):
                total[m] += dot(w, high[m, upper])

    rounded = total[...].astype(bf16)
    lat_out[...] = rounded
    cells = rounded.shape[1]
    pre = dot(w_in[...], rounded.reshape(members * cells, -1), NT)
    _, half = gelu_parts(pre)
    out = dot(w_out[...], (pre * half).astype(bf16))
    for m in range(members):
        fields[m] = out[:, m * cells : (m + 1) * cells].astype(bf16)


def slopes_kernel(lat, w_in, act_t, slope_t):
    members, cells = lat.shape[0], lat.shape[1]
    x = dot(w_in[...], lat[...].reshape(members * cells, -1), NT)
    square, half = gelu_parts(x)
    scale = 0.7978845608028654
    act = (x * half).astype(bf16)
    inner = x * (2.0 * scale + (6.0 * scale * 0.044715) * square)
    slope = (half + half * (1.0 - half) * inner).astype(bf16)
    for m in range(members):
        act_t[m] = act[:, m * cells : (m + 1) * cells]
        slope_t[m] = slope[:, m * cells : (m + 1) * cells]


def smooth_sign(u):
    return u * lax.rsqrt(u * u + smooth_square)


def weights_kernel(
    place, own, other1, other2, other3, target, area, var_weight, act_t, slope_t, lat, w_out_t,
    grad_pre, keep, send, total_in, total_out, *, ensemble, states,
):
    step = pl.program_id(0)
    members = own.shape[0]
    truth = target[...].astype(f32)
    mine = [own[m].astype(f32) for m in range(members)]
    spread = [jnp.zeros_like(truth) for _ in mine]
    for a in range(members):
        for b in range(a + 1, members):
            d = smooth_sign(mine[a] - mine[b])
            spread[a] += d
            spread[b] -= d
    for other in (other1, other2, other3):
        for b in range(members):
            theirs = other[b].astype(f32)
            for a in range(members):
                spread[a] += smooth_sign(mine[a] - theirs)
    cell_weight = area[...] * var_weight[...] * (1.0 / states)
    cots = []
    for m in range(members):
        value = smooth_sign(mine[m] - truth) * (1.0 / ensemble)
        value = value - spread[m] * (1.0 / (ensemble * (ensemble - 1)))
        cots.append((cell_weight * value).astype(bf16))
    cot = jnp.concatenate(cots, axis=1)
    width = cots[0].shape[1]
    grad_act = dot(w_out_t[...], cot)
    act = jnp.concatenate([act_t[m] for m in range(members)], axis=1)
    slope = jnp.concatenate([slope_t[m] for m in range(members)], axis=1)
    pre = (grad_act * slope.astype(f32)).astype(bf16)
    for m in range(members):
        grad_pre[m] = pre[:, m * width : (m + 1) * width]
    part_in = dot(pre, lat[...].reshape(members * width, -1))
    part_out = dot(act, cot, NT)

    @pl.when(step == 0)
    def _():
        total_in[...] = part_in
        total_out[:, : part_out.shape[1]] = part_out
        total_out[:, part_out.shape[1] :] = jnp.zeros(
            (part_out.shape[0], total_out.shape[1] - part_out.shape[1]), f32
        )

    @pl.when(step > 0)
    def _():
        total_in[...] += part_in
        total_out[:, : part_out.shape[1]] += part_out

    @pl.when(step == pl.num_programs(0) - 1)
    def _():
        rows = keep.shape[0]
        wide = total_in.shape[1]
        stay = pl.multiple_of(place[0] * rows, rows)
        leave = pl.multiple_of((1 - place[0]) * rows, rows)
        keep[:, :wide] = total_in[pl.ds(stay, rows)]
        keep[:, wide:] = total_out[pl.ds(stay, rows)]
        send[:, :wide] = total_in[pl.ds(leave, rows)].astype(bf16)
        send[:, wide:] = total_out[pl.ds(leave, rows)].astype(bf16)


def rim_kernel(ids, count, grad_pre, weight_t, w_in_t, grad_grid, low, high, total):
    t = pl.program_id(0)
    members, cells = grad_pre.shape[0], grad_pre.shape[2]
    slots = weight_t.shape[1]

    @pl.when(t == 0)
    def _():
        total[...] = jnp.zeros_like(total)

    both = jnp.concatenate([grad_pre[m] for m in range(members)], axis=1)
    grid = dot(w_in_t[...], both).astype(bf16)
    for m in range(members):
        grad_grid[m] = grid[:, m * cells : (m + 1) * cells]
    for k in range(slots):
        e = ids[t, k]
        outside = (e < HALO) | (e >= HALO + lat_blocks)
        slot = jnp.where(e < HALO, e, e - lat_blocks)

        @pl.when((k < count[t]) & outside)
        def _():
            w = weight_t[0, k]
            for m in range(members):
                total[slot, m] += dot(w, grad_grid[m], NT)

    @pl.when(t == pl.num_programs(0) - 1)
    def _():
        for m in range(members):
            for e in range(HALO):
                low[m, e] = total[e, m].astype(bf16)
                high[m, e] = total[HALO + e, m].astype(bf16)


def owned_kernel(ids, count, grad_grid, weight_t, out):
    members, tiles = out.shape[0], weight_t.shape[0]
    slots, cells = weight_t.shape[1], weight_t.shape[3]
    blocks = out.shape[1]

    def clear(b, carry):
        for m in range(members):
            out[m, b] = jnp.zeros(out.shape[2:], f32)
        return carry

    lax.fori_loop(0, blocks, clear, 0)

    def tile(t, carry):
        at = pl.ds(pl.multiple_of(t * cells, cells), cells)
        for k in range(slots):
            e = ids[t, k] - HALO

            @pl.when((k < count[t]) & (e >= 0) & (e < blocks))
            def _():
                w = weight_t[t, k]
                for m in range(members):
                    out[m, e] += dot(w, grad_grid[m, :, at], NT)

        return carry

    lax.fori_loop(0, tiles, tile, 0)


def add_rim_kernel(base, below, above, out):
    side = pl.program_id(0)

    @pl.when(side == 0)
    def _():
        out[...] = base[...] + below[...].astype(f32)

    @pl.when(side == 1)
    def _():
        out[...] = base[...] + above[...].astype(f32)


def split_kernel(place, kept, *refs, which, received):
    got, outs = refs[:received], refs[received : received + 4]
    total = refs[received + 4]
    value = kept[...]
    for r in got:
        value = value + r[...].astype(f32)
    parts = total.shape[0]
    rows = total.shape[1]
    for p in range(parts):
        total[p] = value[p * rows : (p + 1) * rows]
    here = place[which]
    for d in range(parts):
        outs[d][...] = total[lax.rem(here + d, parts)].astype(outs[d].dtype)


def split(place, which, kept, got, dtype):
    parts = 4
    rows, wide = kept.shape[0] // parts, kept.shape[1]
    return pl.pallas_call(
        functools.partial(split_kernel, which=which, received=len(got)),
        in_specs=[smem()] + [whole()] * (1 + len(got)),
        out_specs=[whole()] * parts,
        out_shape=[shape((rows, wide), f32)] + [shape((rows, wide), dtype)] * (parts - 1),
        scratch_shapes=[pltpu.VMEM((parts, rows, wide), f32)],
        compiler_params=params(8),
        cost_estimate=cost(kept.size, kept.size * 8),
    )(place, kept, *got)


def finish_kernel(kept, got1, got2, got3, grad_in, grad_out):
    value = kept[...] + got1[...] + got2[...] + got3[...]
    wide = grad_in.shape[1]
    grad_in[...] = value[:, :wide]
    turned = value[:, wide:].T
    grad_out[...] = turned[: grad_out.shape[0]]


def shift(count, distance):
    return [(i, (i + distance) % count) for i in range(count)]


def shift_y(side_y, side_z, distance):
    return [
        (y * side_z + z, (y + distance) % side_y * side_z + z)
        for y in range(side_y)
        for z in range(side_z)
    ]


def shift_z(side_y, side_z, distance):
    return [
        (y * side_z + z, y * side_z + (z + distance) % side_z)
        for y in range(side_y)
        for z in range(side_z)
    ]


def local(latents, edge_weight, block_ids, block_count, w_in, w_out, targets, area, var_weight):
    members = latents.shape[1]
    feature = latents.shape[3]
    hidden = w_in.shape[0]
    variables = w_out.shape[0]
    rows_v = (variables + 7) // 8 * 8
    tiles, slots, cells, nodes = edge_weight.shape
    count_cells = tiles * cells
    lat = latents[0].reshape(members, -1, nodes, feature)
    blocks = lat.shape[1]
    space = lax.axis_size("space")
    side = 4
    at_space = lax.axis_index("space")
    place = jnp.stack(
        [lax.axis_index("dp"), lax.axis_index("member"), at_space // side, at_space % side]
    ).astype(jnp.int32)

    up = [(i, i + 1) for i in range(space - 1)]
    down = [(i + 1, i) for i in range(space - 1)]
    low = lax.ppermute(lat[:, blocks - HALO :], "space", up)
    high = lax.ppermute(lat[:, :HALO], "space", down)

    w_out_pad = jnp.pad(w_out, ((0, rows_v - variables), (0, 0)))
    target = jnp.pad(targets[0], ((0, rows_v - variables), (0, 0)))
    scale_v = jnp.pad(var_weight, (0, rows_v - variables))[:, None]
    scale_n = area[None, :]

    acc, weight_t, w_in_t, w_out_t = pl.pallas_call(
        own_part_kernel,
        in_specs=[smem(), smem()] + [whole()] * 4,
        out_specs=[whole()] * 4,
        out_shape=[
            shape((members, tiles, cells, feature), f32),
            shape((tiles, slots, nodes, cells), bf16),
            shape((feature, hidden), bf16),
            shape((hidden, rows_v), bf16),
        ],
        compiler_params=params(24),
        cost_estimate=cost(2 * tiles * slots * cells * nodes * feature * members, 10 * MIB),
    )(block_ids, block_count, lat, edge_weight, w_in, w_out_pad)

    lat_spec = pl.BlockSpec((members, cells, feature), lambda t: (0, t, 0))
    col_spec = pl.BlockSpec((members, hidden, cells), lambda t: (0, 0, t))
    grid_latent, fields = pl.pallas_call(
        fields_kernel,
        grid=(tiles,),
        in_specs=[
            smem(),
            smem(),
            pl.BlockSpec((members, 1, cells, feature), lambda t: (0, t, 0, 0)),
            whole(),
            whole(),
            pl.BlockSpec((1, slots, cells, nodes), lambda t: (t, 0, 0, 0)),
            whole(),
            whole(),
        ],
        out_specs=[lat_spec, pl.BlockSpec((members, rows_v, cells), lambda t: (0, 0, t))],
        out_shape=[
            shape((members, count_cells, feature), bf16),
            shape((members, rows_v, count_cells), bf16),
        ],
        scratch_shapes=[pltpu.VMEM((members, cells, feature), f32)],
        compiler_params=params(16),
        cost_estimate=cost(2 * members * count_cells * feature * hidden, 8 * MIB),
    )(block_ids, block_count, acc, low, high, edge_weight, w_in, w_out_pad)

    ring = lax.axis_size("member")
    others = [lax.ppermute(fields, "member", shift(ring, d)) for d in (1, 3, 2)]

    act_t, slope_t = pl.pallas_call(
        slopes_kernel,
        grid=(tiles,),
        in_specs=[lat_spec, whole()],
        out_specs=[col_spec, col_spec],
        out_shape=[shape((members, hidden, count_cells), bf16)] * 2,
        compiler_params=params(16),
        cost_estimate=cost(2 * members * count_cells * feature * hidden, 8 * MIB),
    )(grid_latent, w_in)

    width = 2 * cells
    wide = feature + 128
    field_spec = pl.BlockSpec((members, rows_v, width), lambda t: (0, 0, t))
    wide_spec = pl.BlockSpec((members, hidden, width), lambda t: (0, 0, t))
    half_rows = hidden // 2
    grad_pre, keep, send = pl.pallas_call(
        functools.partial(
            weights_kernel, ensemble=members * ring, states=targets.shape[0] * lax.axis_size("dp")
        ),
        grid=(count_cells // width,),
        in_specs=[
            smem(),
            field_spec,
            field_spec,
            field_spec,
            field_spec,
            pl.BlockSpec((rows_v, width), lambda t: (0, t)),
            pl.BlockSpec((1, width), lambda t: (0, t)),
            whole(),
            wide_spec,
            wide_spec,
            pl.BlockSpec((members, width, feature), lambda t: (0, t, 0)),
            whole(),
        ],
        out_specs=[wide_spec, whole(), whole()],
        out_shape=[
            shape((members, hidden, count_cells), bf16),
            shape((half_rows, wide), f32),
            shape((half_rows, wide), bf16),
        ],
        scratch_shapes=[pltpu.VMEM((hidden, feature), f32), pltpu.VMEM((hidden, 128), f32)],
        compiler_params=params(24),
        cost_estimate=cost(2 * members * count_cells * feature * hidden, 8 * MIB),
    )(place, fields, *others, target, scale_n, scale_v, act_t, slope_t, grid_latent, w_out_t)

    swapped = lax.ppermute(send, "dp", [(0, 1), (1, 0)])

    grad_grid, rim_low, rim_high = pl.pallas_call(
        rim_kernel,
        grid=(tiles,),
        in_specs=[
            smem(),
            smem(),
            col_spec,
            pl.BlockSpec((1, slots, nodes, cells), lambda t: (t, 0, 0, 0)),
            whole(),
        ],
        out_specs=[col_spec, whole(), whole()],
        out_shape=[
            shape((members, feature, count_cells), bf16),
            shape((members, HALO, nodes, feature), bf16),
            shape((members, HALO, nodes, feature), bf16),
        ],
        scratch_shapes=[pltpu.VMEM((2 * HALO, members, nodes, feature), f32)],
        compiler_params=params(16),
        cost_estimate=cost(2 * members * count_cells * feature * hidden, 6 * MIB),
    )(block_ids, block_count, grad_pre, weight_t, w_in_t)

    from_below = lax.ppermute(rim_high, "space", up)
    from_above = lax.ppermute(rim_low, "space", down)

    owned = pl.pallas_call(
        owned_kernel,
        in_specs=[smem(), smem(), whole(), whole()],
        out_specs=whole(),
        out_shape=shape((members, blocks, nodes, feature), f32),
        compiler_params=params(24),
        cost_estimate=cost(2 * tiles * slots * cells * nodes * feature * members, 12 * MIB),
    )(block_ids, block_count, grad_grid, weight_t)

    kept, *sends = split(place, 1, keep, [swapped], bf16)
    got = [
        lax.ppermute(s, "member", shift(ring, d)) for d, s in zip((1, 2, 3), sends)
    ]
    kept, *sends = split(place, 2, kept, got, f32)
    got = [lax.ppermute(s, "space", shift_y(side, side, d)) for d, s in zip((1, 2, 3), sends)]
    kept, *sends = split(place, 3, kept, got, f32)
    got = [lax.ppermute(s, "space", shift_z(side, side, d)) for d, s in zip((1, 2, 3), sends)]
    grad_w_in, grad_w_out = pl.pallas_call(
        finish_kernel,
        in_specs=[whole()] * 4,
        out_specs=[whole()] * 2,
        out_shape=[
            shape((kept.shape[0], feature), f32),
            shape((variables, kept.shape[0]), f32),
        ],
        compiler_params=params(8),
    )(kept, *got)

    rim_spec = pl.BlockSpec((1, HALO, nodes, feature), lambda s, m: (m, 0, 0, 0))
    last = blocks // HALO - 1
    edge_spec = pl.BlockSpec((1, HALO, nodes, feature), lambda s, m: (m, s * last, 0, 0))
    grad_latent = pl.pallas_call(
        add_rim_kernel,
        grid=(2, members),
        in_specs=[edge_spec, rim_spec, rim_spec],
        out_specs=edge_spec,
        out_shape=shape(owned.shape, f32),
        input_output_aliases={0: 0},
        compiler_params=params(16),
    )(owned, from_below, from_above)
    return (
        grad_latent.reshape(1, members, blocks * nodes, feature),
        grad_w_in,
        grad_w_out,
    )


def solution(mesh):
    placed = (
        P("dp", "member", "space", None),
        P("space", None, None, None),
        P("space", None),
        P("space"),
        P(),
        P(),
        P("dp", None, "space"),
        P("space"),
        P(),
    )
    return jax.shard_map(
        local,
        mesh=mesh,
        in_specs=placed,
        out_specs=(
            P("dp", "member", "space", None),
            P(("dp", "member", "space"), None),
            P(None, ("dp", "member", "space")),
        ),
        check_vma=False,
    )
```

```python
import functools

import jax
import jax.numpy as jnp
from jax import lax
from jax.experimental import pallas as pl
from jax.experimental.pallas import tpu as pltpu
from jax.sharding import PartitionSpec as P

HALO = 2
smooth_square = 0.1 * 0.1
gelu_scale = 0.7978845608028654
gelu_cubic = 0.044715
MIB = 1 << 20
f32 = jnp.float32
bf16 = jnp.bfloat16

NN = (((1,), (0,)), ((), ()))
NT = (((1,), (1,)), ((), ()))


def dot(a, b, dims=NN):
    return lax.dot_general(a, b, dims, preferred_element_type=f32)


def vmem():
    return pl.BlockSpec(memory_space=pltpu.VMEM)


def smem():
    return pl.BlockSpec(memory_space=pltpu.SMEM)


def hbm():
    return pl.BlockSpec(memory_space=pltpu.HBM)


def in_hbm(x):
    return pltpu.with_memory_space_constraint(x, pltpu.HBM)


def in_vmem(*xs):
    return [pltpu.with_memory_space_constraint(x, pltpu.VMEM) for x in xs]


def held(dims, dtype):
    return pltpu.VMEM(dims, dtype)


def anywhere():
    return pl.BlockSpec(memory_space=pl.ANY)


def cost(flops, moved, transcendentals=0):
    return pl.CostEstimate(
        flops=int(flops), bytes_accessed=int(moved), transcendentals=int(transcendentals)
    )


def params(mib):
    return pltpu.CompilerParams(vmem_limit_bytes=mib * MIB)


def shape(dims, dtype):
    return jax.ShapeDtypeStruct(dims, dtype)


def rows_at(start, size):
    return pl.ds(pl.multiple_of(start * size, size), size)


def prepare_kernel(
    meta, lat_hbm, weight_hbm, w_in_hbm, w_out,
    acc0, acc1, halo_w, halo_wt, own_wt, w_in_v, w_in_t, w_out_v, w_out_t,
    lat, weight, sems, *, spaces,
):
    tiles, slots, cells, nodes = weight.shape
    members, blocks = lat.shape[0], lat.shape[1]
    copies = [
        pltpu.make_async_copy(weight_hbm, weight, sems.at[0]),
        pltpu.make_async_copy(lat_hbm.at[0], lat.at[0], sems.at[1]),
        pltpu.make_async_copy(lat_hbm.at[1], lat.at[1], sems.at[2]),
        pltpu.make_async_copy(w_in_hbm, w_in_v, sems.at[3]),
    ]
    for c in copies:
        c.start()
    at_space = meta[tiles * slots + tiles]
    halo_w[...] = jnp.zeros_like(halo_w)
    halo_wt[...] = jnp.zeros_like(halo_wt)
    own_wt[...] = jnp.zeros_like(own_wt)
    copies[0].wait()

    def place_tile(t, carry):
        for k in range(slots):
            e = meta[k * tiles + t]
            live = k < meta[slots * tiles + t]
            w = weight[t, k]
            wt = w.T
            below = (e < HALO) & (at_space > 0)
            above = (e >= HALO + blocks) & (at_space < spaces - 1)
            mine = (e >= HALO) & (e < HALO + blocks)
            slot = jnp.where(e < HALO, e, jnp.where(mine, 0, e - blocks))
            block = jnp.clip(e - HALO, 0, blocks - 1)

            @pl.when(live & (below | above))
            def _():
                halo_w[rows_at(t, cells), rows_at(slot, nodes)] += w
                halo_wt[rows_at(slot, nodes), rows_at(t, cells)] += wt

            @pl.when(live & mine)
            def _():
                own_wt[rows_at(block, nodes), rows_at(t, cells)] += wt

        return carry

    lax.fori_loop(0, tiles, place_tile, 0)
    for c in copies[1:]:
        c.wait()

    def gather_tile(t, carry):
        parts, at = [], []
        for k in range(slots):
            e = meta[k * tiles + t]
            mine = (k < meta[slots * tiles + t]) & (e >= HALO) & (e < HALO + blocks)
            w = weight[t, k]
            parts.append(jnp.where(mine, w, jnp.zeros_like(w)))
            at.append(jnp.clip(e - HALO, 0, blocks - 1))
        lhs = jnp.concatenate(parts, axis=1)
        for m, acc in enumerate((acc0, acc1)):
            rhs = jnp.concatenate([lat[m, a] for a in at], axis=0)
            acc[rows_at(t, cells)] = dot(lhs, rhs)
        return carry

    lax.fori_loop(0, tiles, gather_tile, 0)
    w_in_t[...] = w_in_v[...].T
    variables = w_out.shape[0]
    w_out_v[...] = jnp.zeros_like(w_out_v)
    w_out_v[:variables] = w_out[...]
    w_out_t[...] = w_out_v[...].T


def gelu_parts(x):
    square = x * x
    half = 0.5 + 0.5 * jnp.tanh(x * (gelu_scale + (gelu_scale * gelu_cubic) * square))
    return square, half


CHUNK = 256


def fields_kernel(acc, low, high, halo_w, w_in, w_out, lat_out, fields):
    count = acc.shape[0]
    half_k = low.shape[0]
    for start in range(0, count, 2 * CHUNK):
        at = slice(start, start + 2 * CHUNK)
        total = acc[at] + dot(halo_w[at, :half_k], low[...])
        total = total + dot(halo_w[at, half_k:], high[...])
        rounded = total.astype(bf16)
        lat_out[at] = rounded
        pre = dot(w_in[...], rounded, NT)
        _, half = gelu_parts(pre)
        fields[:, at] = dot(w_out[...], (pre * half).astype(bf16)).astype(bf16)


def slopes_kernel(lat, w_in, act_t, slope_t):
    count = lat.shape[0]
    for start in range(0, count, CHUNK):
        at = slice(start, start + CHUNK)
        x = dot(w_in[...], lat[at], NT)
        square, half = gelu_parts(x)
        act_t[:, at] = (x * half).astype(bf16)
        inner = x * (2.0 * gelu_scale + (6.0 * gelu_scale * gelu_cubic) * square)
        slope_t[:, at] = (half + half * (1.0 - half) * inner).astype(bf16)


def smooth_sign(u):
    return u * lax.rsqrt(u * u + smooth_square)


def weights_kernel(
    meta, own0, own1, o10, o11, o20, o21, o30, o31, target, area, var_weight,
    act0, act1, slope0, slope1, lat0, lat1, w_out_t,
    grad_pre0, grad_pre1, keep, send, total_in, total_out, *, ensemble, states, dp_at,
):
    count = own0.shape[1]
    others = (o10, o11, o20, o21, o30, o31)
    for start in range(0, count, CHUNK):
        at = slice(start, start + CHUNK)
        truth = target[:, at].astype(f32)
        mine = [own0[:, at].astype(f32), own1[:, at].astype(f32)]
        pair = smooth_sign(mine[0] - mine[1])
        spread = [pair, -pair]
        for other in others:
            theirs = other[:, at].astype(f32)
            for a in range(2):
                spread[a] = spread[a] + smooth_sign(mine[a] - theirs)
        cell_weight = area[:, at] * var_weight[...] * (1.0 / states)
        cots = []
        for a in range(2):
            value = smooth_sign(mine[a] - truth) * (1.0 / ensemble)
            value = value - spread[a] * (1.0 / (ensemble * (ensemble - 1)))
            cots.append((cell_weight * value).astype(bf16))
        cot = jnp.concatenate(cots, axis=1)
        grad_act = dot(w_out_t[...], cot)
        slope = jnp.concatenate([slope0[:, at], slope1[:, at]], axis=1)
        pre = (grad_act * slope.astype(f32)).astype(bf16)
        grad_pre0[:, at] = pre[:, :CHUNK]
        grad_pre1[:, at] = pre[:, CHUNK:]
        part_in = dot(pre, jnp.concatenate([lat0[at], lat1[at]], axis=0))
        act = jnp.concatenate([act0[:, at], act1[:, at]], axis=1)
        part_out = dot(act, cot, NT)
        if start == 0:
            total_in[...] = part_in
            total_out[...] = jnp.zeros_like(total_out)
            total_out[:, : part_out.shape[1]] = part_out
        else:
            total_in[...] += part_in
            total_out[:, : part_out.shape[1]] += part_out
    rows = keep.shape[0]
    wide = total_in.shape[1]
    here = meta[dp_at]
    stay, leave = rows_at(here, rows), rows_at(1 - here, rows)
    keep[:, :wide] = total_in[stay]
    keep[:, wide:] = total_out[stay]
    send[:, :wide] = total_in[leave].astype(bf16)
    send[:, wide:] = total_out[leave].astype(bf16)


def rim_kernel(grad_pre0, grad_pre1, halo_wt, w_in_t, grad_grid0, grad_grid1, low, high):
    half_k = low.shape[1]
    for m, (grad_pre, grad_grid) in enumerate(
        ((grad_pre0, grad_grid0), (grad_pre1, grad_grid1))
    ):
        grad_grid[...] = dot(w_in_t[...], grad_pre[...]).astype(bf16)
        low[m] = dot(halo_wt[:half_k], grad_grid[...], NT).astype(bf16)
        high[m] = dot(halo_wt[half_k:], grad_grid[...], NT).astype(bf16)


def owned_kernel(grad_grid0, grad_grid1, own_wt, out, edge, parts, sems):
    step = edge.shape[2]
    count = own_wt.shape[0] // step
    copies = []
    for m, grad_grid in enumerate((grad_grid0, grad_grid1)):
        for i in range(count):
            value = dot(own_wt[i * step : (i + 1) * step], grad_grid[...], NT)
            if i == 0:
                edge[m, 0] = value
            elif i == count - 1:
                edge[m, 1] = value
            else:
                slot = len(copies)
                parts[slot] = value
                copy = pltpu.make_async_copy(
                    parts.at[slot], out.at[m, i * step : (i + 1) * step], sems.at[slot]
                )
                copy.start()
                copies.append(copy)
    for copy in copies:
        copy.wait()


def add_rim_kernel(base, edge, below, above, out, parts, sems):
    step = edge.shape[2]
    last = out.shape[1] - step
    copies = []
    for side, (start, got) in enumerate(((0, below), (last, above))):
        for m in range(edge.shape[0]):
            slot = side * edge.shape[0] + m
            parts[slot] = edge[m, side] + got[m].astype(f32)
            copy = pltpu.make_async_copy(
                parts.at[slot], out.at[m, start : start + step], sems.at[slot]
            )
            copy.start()
            copies.append(copy)
    for copy in copies:
        copy.wait()


def split_kernel(meta, kept, swapped, own, send1, send2, send3, total, *, member_at):
    parts, rows = total.shape[0], total.shape[1]
    value = kept[...] + swapped[...].astype(f32)
    for p in range(parts):
        total[p] = value[p * rows : (p + 1) * rows]
    here = meta[member_at]
    own[...] = total[here]
    for d, out in ((1, send1), (2, send2), (3, send3)):
        out[...] = total[lax.rem(here + d, parts)].astype(out.dtype)


def scatter_kernel(kept, got1, got2, got3, later, out):
    value = kept[...] + got1[...].astype(f32) + got2[...].astype(f32) + got3[...].astype(f32)
    parts, rows = out.shape[0], out.shape[1]
    for p in range(parts):
        out[p] = value[p * rows : (p + 1) * rows].astype(out.dtype)


def finish_kernel(got, grad_in, grad_out):
    value = got[0].astype(f32)
    for p in range(1, got.shape[0]):
        value = value + got[p].astype(f32)
    wide = grad_in.shape[1]
    grad_in[...] = value[:, :wide]
    grad_out[...] = value[:, wide : wide + grad_out.shape[1]]


def ring(count, distance):
    return [(i, (i + distance) % count) for i in range(count)]


def local(latents, edge_weight, block_ids, block_count, w_in, w_out, targets, area, var_weight):
    members = latents.shape[1]
    feature = latents.shape[3]
    hidden = w_in.shape[0]
    variables = w_out.shape[0]
    rows_v = (variables + 7) // 8 * 8
    tiles, slots, cells, nodes = edge_weight.shape
    n = tiles * cells
    lat = latents[0].reshape(members, -1, nodes, feature)
    blocks = lat.shape[1]
    edge_rows = HALO * nodes
    rim_rows = 2 * edge_rows
    spaces = lax.axis_size("space")
    chips = lax.axis_size("member")
    meta = jnp.concatenate(
        [
            block_ids.T.reshape(-1),
            block_count,
            jnp.stack(
                [lax.axis_index("space"), lax.axis_index("dp"), lax.axis_index("member")]
            ).astype(jnp.int32),
        ]
    )
    dp_at = tiles * slots + tiles + 1
    member_at = dp_at + 1

    flat = latents[0]
    halos = []
    for m in range(members):
        low = lax.ppermute(flat[m, -edge_rows:], "space", ring(spaces, 1))
        high = lax.ppermute(flat[m, :edge_rows], "space", ring(spaces, -1))
        halos.append((low, high))

    target = jnp.pad(targets[0], ((0, rows_v - variables), (0, 0)))
    scale_v = jnp.pad(var_weight, (0, rows_v - variables))[:, None]
    scale_n = area[None, :]

    acc0, acc1, halo_w, halo_wt, own_wt, w_in_v, w_in_t, w_out_v, w_out_t = pl.pallas_call(
        functools.partial(prepare_kernel, spaces=spaces),
        in_specs=[smem(), hbm(), hbm(), hbm(), vmem()],
        out_specs=[vmem()] * 9,
        out_shape=[
            held((n, feature), f32),
            held((n, feature), f32),
            held((n, rim_rows), bf16),
            held((rim_rows, n), bf16),
            held((blocks * nodes, n), bf16),
            held((hidden, feature), bf16),
            held((feature, hidden), bf16),
            held((rows_v, hidden), bf16),
            held((hidden, rows_v), bf16),
        ],
        scratch_shapes=[
            pltpu.VMEM(lat.shape, bf16),
            pltpu.VMEM(edge_weight.shape, bf16),
            pltpu.SemaphoreType.DMA((4,)),
        ],
        compiler_params=params(28),
        cost_estimate=cost(2 * n * slots * nodes * feature * members, 10 * MIB),
    )(meta, in_hbm(lat), in_hbm(edge_weight), in_hbm(w_in), w_out)

    grid_latent, fields, acts, slopes = [], [], [], []
    for m, acc in enumerate((acc0, acc1)):
        low, high = halos[m]
        lat_m, fields_m = pl.pallas_call(
            fields_kernel,
            in_specs=[vmem()] * 6,
            out_specs=[vmem()] * 2,
            out_shape=[held((n, feature), bf16), shape((rows_v, n), bf16)],
            compiler_params=params(16),
            cost_estimate=cost(4 * n * feature * hidden, MIB, n * hidden),
        )(*in_vmem(acc), low, high, *in_vmem(halo_w, w_in_v, w_out_v))
        grid_latent.append(lat_m)
        fields.append(fields_m)
        act_m, slope_m = pl.pallas_call(
            slopes_kernel,
            in_specs=[vmem()] * 2,
            out_specs=[vmem()] * 2,
            out_shape=[held((hidden, n), bf16)] * 2,
            compiler_params=params(16),
            cost_estimate=cost(4 * n * feature * hidden, MIB, n * hidden),
        )(*in_vmem(lat_m, w_in_v))
        acts.append(act_m)
        slopes.append(slope_m)

    def along(x, distance):
        return lax.ppermute(x, "member", ring(chips, distance))

    left0 = along(fields[0], 1)
    right0 = along(fields[0], -1)
    far0 = along(left0, 1)
    right1 = along(fields[1], -1)
    left1 = along(fields[1], 1)
    far1 = along(right1, -1)

    wide = feature + 128
    half_rows = hidden // 2
    grad_pre0, grad_pre1, keep, send = pl.pallas_call(
        functools.partial(
            weights_kernel,
            ensemble=members * chips,
            states=targets.shape[0] * lax.axis_size("dp"),
            dp_at=dp_at,
        ),
        in_specs=[smem()] + [vmem()] * 18,
        out_specs=[vmem()] * 4,
        out_shape=[
            held((hidden, n), bf16),
            held((hidden, n), bf16),
            shape((half_rows, wide), f32),
            shape((half_rows, wide), bf16),
        ],
        scratch_shapes=[pltpu.VMEM((hidden, feature), f32), pltpu.VMEM((hidden, 128), f32)],
        compiler_params=params(20),
        cost_estimate=cost(4 * n * feature * hidden, MIB),
    )(
        meta, *fields, left0, left1, right0, right1, far0, far1, target, scale_n, scale_v,
        *in_vmem(*acts, *slopes, *grid_latent, w_out_t),
    )

    swapped = lax.ppermute(send, "dp", [(0, 1), (1, 0)])

    grad_grid0, grad_grid1, rim_low, rim_high = pl.pallas_call(
        rim_kernel,
        in_specs=[vmem()] * 4,
        out_specs=[vmem()] * 4,
        out_shape=[held((feature, n), bf16)] * 2 + [shape((members, edge_rows, feature), bf16)] * 2,
        compiler_params=params(16),
        cost_estimate=cost(8 * n * feature * hidden, MIB),
    )(*in_vmem(grad_pre0, grad_pre1, halo_wt, w_in_t))

    from_below = lax.ppermute(rim_high, "space", ring(spaces, 1))
    from_above = lax.ppermute(rim_low, "space", ring(spaces, -1))

    quarter = half_rows // chips
    kept, *sends = pl.pallas_call(
        functools.partial(split_kernel, member_at=member_at),
        in_specs=[smem(), vmem(), vmem()],
        out_specs=[vmem()] * 4,
        out_shape=[shape((quarter, wide), f32)] + [shape((quarter, wide), bf16)] * 3,
        scratch_shapes=[pltpu.VMEM((chips, quarter, wide), f32)],
        compiler_params=params(8),
    )(meta, keep, swapped)
    got = [along(s, d) for d, s in zip((1, 2, 3), sends)]

    middle = blocks // HALO - 2
    owned, edge = pl.pallas_call(
        owned_kernel,
        in_specs=[vmem()] * 3,
        out_specs=[hbm(), vmem()],
        out_shape=[
            shape((members, blocks * nodes, feature), f32),
            held((members, 2, edge_rows, feature), f32),
        ],
        scratch_shapes=[
            pltpu.VMEM((members * middle, edge_rows, feature), f32),
            pltpu.SemaphoreType.DMA((members * middle,)),
        ],
        compiler_params=params(20),
        cost_estimate=cost(2 * blocks * nodes * n * feature * members, 8 * MIB),
    )(*in_vmem(grad_grid0, grad_grid1, own_wt))

    last_rows = quarter // spaces
    spread = pl.pallas_call(
        scatter_kernel,
        in_specs=[vmem()] * 4 + [anywhere()],
        out_specs=vmem(),
        out_shape=shape((spaces, last_rows, wide), bf16),
        compiler_params=params(8),
    )(kept, *got, edge)
    spread = lax.all_to_all(spread, "space", 0, 0, tiled=True)
    grad_w_in, grad_w_out = pl.pallas_call(
        finish_kernel,
        in_specs=[vmem()],
        out_specs=[vmem()] * 2,
        out_shape=[shape((last_rows, feature), f32), shape((last_rows, variables), f32)],
        compiler_params=params(8),
    )(spread)

    grad_latent = pl.pallas_call(
        add_rim_kernel,
        in_specs=[hbm(), vmem(), vmem(), vmem()],
        out_specs=hbm(),
        out_shape=shape(owned.shape, f32),
        scratch_shapes=[
            pltpu.VMEM((2 * members, edge_rows, feature), f32),
            pltpu.SemaphoreType.DMA((2 * members,)),
        ],
        input_output_aliases={0: 0},
        compiler_params=params(8),
    )(owned, *in_vmem(edge), from_below, from_above)
    return grad_latent[None], grad_w_in, grad_w_out.T


def solution(mesh):
    placed = (
        P("dp", "member", "space", None),
        P("space", None, None, None),
        P("space", None),
        P("space"),
        P(),
        P(),
        P("dp", None, "space"),
        P("space"),
        P(),
    )
    return jax.shard_map(
        local,
        mesh=mesh,
        in_specs=placed,
        out_specs=(
            P("dp", "member", "space", None),
            P(("dp", "member", "space"), None),
            P(None, ("dp", "member", "space")),
        ),
        check_vma=False,
    )
```

```python
import functools

import jax
import jax.numpy as jnp
from jax import lax
from jax.experimental import pallas as pl
from jax.experimental.pallas import tpu as pltpu
from jax.sharding import PartitionSpec as P

HALO = 2
smooth_square = 0.1 * 0.1
gelu_scale = 0.7978845608028654
gelu_cubic = 0.044715
MIB = 1 << 20
f32 = jnp.float32
bf16 = jnp.bfloat16

NN = (((1,), (0,)), ((), ()))
NT = (((1,), (1,)), ((), ()))


def dot(a, b, dims=NN):
    return lax.dot_general(a, b, dims, preferred_element_type=f32)


def vmem():
    return pl.BlockSpec(memory_space=pltpu.VMEM)


def smem():
    return pl.BlockSpec(memory_space=pltpu.SMEM)


def hbm():
    return pl.BlockSpec(memory_space=pltpu.HBM)


def in_hbm(x):
    return pltpu.with_memory_space_constraint(x, pltpu.HBM)


def in_vmem(*xs):
    return [pltpu.with_memory_space_constraint(x, pltpu.VMEM) for x in xs]


def held(dims, dtype):
    return pltpu.VMEM(dims, dtype)


def anywhere():
    return pl.BlockSpec(memory_space=pl.ANY)


def cost(flops, moved, transcendentals=0):
    return pl.CostEstimate(
        flops=int(flops), bytes_accessed=int(moved), transcendentals=int(transcendentals)
    )


def params(mib):
    return pltpu.CompilerParams(vmem_limit_bytes=mib * MIB)


def shape(dims, dtype):
    return jax.ShapeDtypeStruct(dims, dtype)


def rows_at(start, size):
    return pl.ds(pl.multiple_of(start * size, size), size)


def parity():
    return lax.rem(lax.axis_index("space"), 2)


def edges_kernel(lat, near0, far0, near1, far1, sems):
    step = near0.shape[0]
    last = lat.shape[1] - step
    odd = parity()
    top = pl.multiple_of((1 - odd) * last, step)
    bottom = pl.multiple_of(odd * last, step)
    copies = []
    for m, (near, far) in enumerate(((near0, far0), (near1, far1))):
        for out, start in ((near, top), (far, bottom)):
            copies.append(
                pltpu.make_async_copy(lat.at[m, pl.ds(start, step)], out, sems.at[len(copies)])
            )
            copies[-1].start()
    for copy in copies:
        copy.wait()


def halo_slot(e, blocks, spaces):
    at_space = lax.axis_index("space")
    odd = parity()
    below, above = e < HALO, e >= HALO + blocks
    outside = (below & (at_space > 0)) | (above & (at_space < spaces - 1))
    slot = jnp.where(below, e + (1 - odd) * HALO, e - HALO - blocks + odd * HALO)
    return outside, jnp.where(below | above, slot, 0)


def prepare_kernel(
    ids, count, lat_hbm, weight_hbm, w_in_hbm, w_out, acc0, acc1, halo_w, w_in_v, w_out_v,
    lat, weight, sems, *, spaces,
):
    tiles, slots, cells, nodes = weight.shape
    blocks = lat.shape[1]
    copies = [
        pltpu.make_async_copy(weight_hbm, weight, sems.at[0]),
        pltpu.make_async_copy(lat_hbm.at[0], lat.at[0], sems.at[1]),
        pltpu.make_async_copy(lat_hbm.at[1], lat.at[1], sems.at[2]),
        pltpu.make_async_copy(w_in_hbm, w_in_v, sems.at[3]),
    ]
    for c in copies:
        c.start()
    halo_w[...] = jnp.zeros_like(halo_w)
    w_out_v[...] = jnp.zeros_like(w_out_v)
    w_out_v[: w_out.shape[0]] = w_out[...]
    copies[0].wait()

    def place_tile(t, carry):
        for k in range(slots):
            e = ids[k, t]
            outside, slot = halo_slot(e, blocks, spaces)

            @pl.when((k < count[t]) & outside)
            def _():
                halo_w[rows_at(t, cells), rows_at(slot, nodes)] += weight[t, k]

        return carry

    lax.fori_loop(0, tiles, place_tile, 0)

    for m, acc in enumerate((acc0, acc1)):
        copies[1 + m].wait()
        for t in range(tiles):
            parts, at = [], []
            for k in range(slots):
                e = ids[k, t]
                mine = (k < count[t]) & (e >= HALO) & (e < HALO + blocks)
                w = weight[t, k]
                parts.append(jnp.where(mine, w, jnp.zeros_like(w)))
                at.append(jnp.clip(e - HALO, 0, blocks - 1))
            lhs = jnp.concatenate(parts, axis=1)
            rhs = jnp.concatenate([lat[m, a] for a in at], axis=0)
            acc[t * cells : (t + 1) * cells] = dot(lhs, rhs)
    copies[3].wait()


def turn_kernel(
    ids, count, weight_hbm, w_in, w_out, later, halo_wt, own_wt, w_in_t, w_out_t, weight, sems,
    *, spaces,
):
    tiles, slots, cells, nodes = weight.shape
    blocks = own_wt.shape[0] // nodes
    copy = pltpu.make_async_copy(weight_hbm, weight, sems.at[0])
    copy.start()
    halo_wt[...] = jnp.zeros_like(halo_wt)
    own_wt[...] = jnp.zeros_like(own_wt)
    w_in_t[...] = w_in[...].T
    w_out_t[...] = w_out[...].T
    copy.wait()

    def place_tile(t, carry):
        for k in range(slots):
            e = ids[k, t]
            live = k < count[t]
            outside, slot = halo_slot(e, blocks, spaces)
            mine = (e >= HALO) & (e < HALO + blocks)
            block = jnp.clip(e - HALO, 0, blocks - 1)

            @pl.when(live & outside)
            def _():
                halo_wt[rows_at(slot, nodes), rows_at(t, cells)] += weight[t, k].T

            @pl.when(live & mine)
            def _():
                own_wt[rows_at(block, nodes), rows_at(t, cells)] += weight[t, k].T

        return carry

    lax.fori_loop(0, tiles, place_tile, 0)


def gelu_parts(x):
    square = x * x
    half = 0.5 + 0.5 * jnp.tanh(x * (gelu_scale + (gelu_scale * gelu_cubic) * square))
    return square, half


CHUNK = 256


def fields_kernel(acc, near, far, halo_w, w_in, w_out, lat_out, fields):
    count = acc.shape[0]
    half_k = near.shape[0]
    for start in range(0, count, 2 * CHUNK):
        at = slice(start, start + 2 * CHUNK)
        total = acc[at] + dot(halo_w[at, :half_k], near[...])
        total = total + dot(halo_w[at, half_k:], far[...])
        rounded = total.astype(bf16)
        lat_out[at] = rounded
        pre = dot(w_in[...], rounded, NT)
        _, half = gelu_parts(pre)
        fields[:, at] = dot(w_out[...], (pre * half).astype(bf16)).astype(bf16)


def slopes_kernel(lat, w_in, act_t, slope_t):
    count = lat.shape[0]
    for start in range(0, count, CHUNK):
        at = slice(start, start + CHUNK)
        x = dot(w_in[...], lat[at], NT)
        square, half = gelu_parts(x)
        act_t[:, at] = (x * half).astype(bf16)
        inner = x * (2.0 * gelu_scale + (6.0 * gelu_scale * gelu_cubic) * square)
        slope_t[:, at] = (half + half * (1.0 - half) * inner).astype(bf16)


def smooth_sign(u):
    return u * lax.rsqrt(u * u + smooth_square)


def weights_kernel(
    own0, own1, o10, o11, o20, o21, o30, o31, target, area, var_weight,
    act0, act1, slope0, slope1, lat0, lat1, w_out_t,
    grad_pre0, grad_pre1, keep, send, total_in, total_out, *, ensemble, states,
):
    count = own0.shape[1]
    others = (o10, o11, o20, o21, o30, o31)
    for start in range(0, count, CHUNK):
        at = slice(start, start + CHUNK)
        truth = target[:, at].astype(f32)
        mine = [own0[:, at].astype(f32), own1[:, at].astype(f32)]
        pair = smooth_sign(mine[0] - mine[1])
        spread = [pair, -pair]
        for other in others:
            theirs = other[:, at].astype(f32)
            for a in range(2):
                spread[a] = spread[a] + smooth_sign(mine[a] - theirs)
        cell_weight = area[:, at] * var_weight[...] * (1.0 / states)
        cots = []
        for a in range(2):
            value = smooth_sign(mine[a] - truth) * (1.0 / ensemble)
            value = value - spread[a] * (1.0 / (ensemble * (ensemble - 1)))
            cots.append((cell_weight * value).astype(bf16))
        cot = jnp.concatenate(cots, axis=1)
        grad_act = dot(w_out_t[...], cot)
        slope = jnp.concatenate([slope0[:, at], slope1[:, at]], axis=1)
        pre = (grad_act * slope.astype(f32)).astype(bf16)
        grad_pre0[:, at] = pre[:, :CHUNK]
        grad_pre1[:, at] = pre[:, CHUNK:]
        part_in = dot(pre, jnp.concatenate([lat0[at], lat1[at]], axis=0))
        act = jnp.concatenate([act0[:, at], act1[:, at]], axis=1)
        part_out = dot(act, cot, NT)
        if start == 0:
            total_in[...] = part_in
            total_out[...] = jnp.zeros_like(total_out)
            total_out[:, : part_out.shape[1]] = part_out
        else:
            total_in[...] += part_in
            total_out[:, : part_out.shape[1]] += part_out
    rows = keep.shape[0]
    wide = total_in.shape[1]
    here = lax.axis_index("dp")
    stay, leave = rows_at(here, rows), rows_at(1 - here, rows)
    keep[:, :wide] = total_in[stay]
    keep[:, wide:] = total_out[stay]
    send[:, :wide] = total_in[leave].astype(bf16)
    send[:, wide:] = total_out[leave].astype(bf16)


def rim_kernel(grad_pre0, grad_pre1, halo_wt, w_in_t, grad_grid0, grad_grid1, near, far):
    half_k = near.shape[1]
    for m, (grad_pre, grad_grid) in enumerate(
        ((grad_pre0, grad_grid0), (grad_pre1, grad_grid1))
    ):
        grad_grid[...] = dot(w_in_t[...], grad_pre[...]).astype(bf16)
        near[m] = dot(halo_wt[:half_k], grad_grid[...], NT).astype(bf16)
        far[m] = dot(halo_wt[half_k:], grad_grid[...], NT).astype(bf16)


def owned_kernel(grad_grid0, grad_grid1, own_wt, out, edge, parts, sems):
    step = edge.shape[2]
    count = own_wt.shape[0] // step
    copies = []
    for m, grad_grid in enumerate((grad_grid0, grad_grid1)):
        for i in range(count):
            value = dot(own_wt[i * step : (i + 1) * step], grad_grid[...], NT)
            if i == 0:
                edge[m, 0] = value
            elif i == count - 1:
                edge[m, 1] = value
            else:
                slot = len(copies)
                parts[slot] = value
                copy = pltpu.make_async_copy(
                    parts.at[slot], out.at[m, i * step : (i + 1) * step], sems.at[slot]
                )
                copy.start()
                copies.append(copy)
    for copy in copies:
        copy.wait()


def add_rim_kernel(base, edge, near, far, out, parts, sems):
    step = edge.shape[2]
    last = out.shape[1] - step
    odd = parity()
    copies = []
    for side, got in ((1 - odd, near), (odd, far)):
        start = pl.multiple_of(side * last, step)
        for m in range(edge.shape[0]):
            slot = len(copies)
            parts[slot] = edge[m, side] + got[m].astype(f32)
            copy = pltpu.make_async_copy(
                parts.at[slot], out.at[m, pl.ds(start, step)], sems.at[slot]
            )
            copy.start()
            copies.append(copy)
    for copy in copies:
        copy.wait()


def split_kernel(kept, swapped, own, send1, send2, send3, total):
    parts, rows = total.shape[0], total.shape[1]
    value = kept[...] + swapped[...].astype(f32)
    for p in range(parts):
        total[p] = value[p * rows : (p + 1) * rows]
    here = lax.axis_index("member")
    own[...] = total[here]
    for d, out in ((1, send1), (2, send2), (3, send3)):
        out[...] = total[lax.rem(here + d, parts)].astype(out.dtype)


def scatter_kernel(kept, got1, got2, got3, later, out):
    value = kept[...] + got1[...].astype(f32) + got2[...].astype(f32) + got3[...].astype(f32)
    parts, rows = out.shape[0], out.shape[1]
    for p in range(parts):
        out[p] = value[p * rows : (p + 1) * rows].astype(out.dtype)


def finish_kernel(got, grad_in, grad_out):
    value = got[0].astype(f32)
    for p in range(1, got.shape[0]):
        value = value + got[p].astype(f32)
    wide = grad_in.shape[1]
    grad_in[...] = value[:, :wide]
    grad_out[...] = value[:, wide : wide + grad_out.shape[1]]


def ring(count, distance):
    return [(i, (i + distance) % count) for i in range(count)]


def local(latents, edge_weight, block_ids, block_count, w_in, w_out, targets, area, var_weight):
    members = latents.shape[1]
    feature = latents.shape[3]
    hidden = w_in.shape[0]
    variables = w_out.shape[0]
    rows_v = (variables + 7) // 8 * 8
    tiles, slots, cells, nodes = edge_weight.shape
    n = tiles * cells
    lat = latents[0].reshape(members, -1, nodes, feature)
    blocks = lat.shape[1]
    edge_rows = HALO * nodes
    rim_rows = 2 * edge_rows
    spaces = lax.axis_size("space")
    chips = lax.axis_size("member")
    ids = block_ids.T
    first = [(i, i ^ 1) for i in range(spaces)]
    second = [(i, ((i + 1) ^ 1) - 1) for i in range(spaces)]
    second = [(i, j % spaces) for i, j in second]

    edges = pl.pallas_call(
        edges_kernel,
        in_specs=[hbm()],
        out_specs=[vmem()] * 4,
        out_shape=[shape((edge_rows, feature), bf16)] * 4,
        scratch_shapes=[pltpu.SemaphoreType.DMA((4,))],
        compiler_params=params(8),
    )(in_hbm(latents[0]))
    halos = []
    for m in range(members):
        near = lax.ppermute(edges[2 * m], "space", first)
        far = lax.ppermute(edges[2 * m + 1], "space", second)
        halos.append((near, far))

    target = jnp.pad(targets[0], ((0, rows_v - variables), (0, 0)))
    scale_v = jnp.pad(var_weight, (0, rows_v - variables))[:, None]
    scale_n = area[None, :]

    acc0, acc1, halo_w, w_in_v, w_out_v = pl.pallas_call(
        functools.partial(prepare_kernel, spaces=spaces),
        in_specs=[smem(), smem(), hbm(), hbm(), hbm(), vmem()],
        out_specs=[vmem()] * 5,
        out_shape=[
            held((n, feature), f32),
            held((n, feature), f32),
            held((n, rim_rows), bf16),
            held((hidden, feature), bf16),
            held((rows_v, hidden), bf16),
        ],
        scratch_shapes=[
            pltpu.VMEM(lat.shape, bf16),
            pltpu.VMEM(edge_weight.shape, bf16),
            pltpu.SemaphoreType.DMA((4,)),
        ],
        compiler_params=params(24),
        cost_estimate=cost(2 * n * slots * nodes * feature * members, 10 * MIB),
    )(ids, block_count, in_hbm(lat), in_hbm(edge_weight), in_hbm(w_in), in_hbm(w_out))

    grid_latent, fields, acts, slopes = [], [], [], []
    for m, acc in enumerate((acc0, acc1)):
        near, far = halos[m]
        lat_m, fields_m = pl.pallas_call(
            fields_kernel,
            in_specs=[vmem()] * 6,
            out_specs=[vmem()] * 2,
            out_shape=[held((n, feature), bf16), shape((rows_v, n), bf16)],
            compiler_params=params(16),
            cost_estimate=cost(4 * n * feature * hidden, MIB, n * hidden),
        )(*in_vmem(acc), near, far, *in_vmem(halo_w, w_in_v, w_out_v))
        grid_latent.append(lat_m)
        fields.append(fields_m)
        act_m, slope_m = pl.pallas_call(
            slopes_kernel,
            in_specs=[vmem()] * 2,
            out_specs=[vmem()] * 2,
            out_shape=[held((hidden, n), bf16)] * 2,
            compiler_params=params(16),
            cost_estimate=cost(4 * n * feature * hidden, MIB, n * hidden),
        )(*in_vmem(lat_m, w_in_v))
        acts.append(act_m)
        slopes.append(slope_m)

    halo_wt, own_wt, w_in_t, w_out_t = pl.pallas_call(
        functools.partial(turn_kernel, spaces=spaces),
        in_specs=[smem(), smem(), hbm(), vmem(), vmem(), anywhere()],
        out_specs=[vmem()] * 4,
        out_shape=[
            held((rim_rows, n), bf16),
            held((blocks * nodes, n), bf16),
            held((feature, hidden), bf16),
            held((hidden, rows_v), bf16),
        ],
        scratch_shapes=[pltpu.VMEM(edge_weight.shape, bf16), pltpu.SemaphoreType.DMA((1,))],
        compiler_params=params(16),
        cost_estimate=cost(MIB, 6 * MIB),
    )(ids, block_count, in_hbm(edge_weight), *in_vmem(w_in_v, w_out_v), fields[1])

    def along(x, distance):
        return lax.ppermute(x, "member", ring(chips, distance))

    left0 = along(fields[0], 1)
    right0 = along(fields[0], -1)
    far0 = along(left0, 1)
    right1 = along(fields[1], -1)
    left1 = along(fields[1], 1)
    far1 = along(right1, -1)

    wide = feature + 128
    half_rows = hidden // 2
    grad_pre0, grad_pre1, keep, send = pl.pallas_call(
        functools.partial(
            weights_kernel,
            ensemble=members * chips,
            states=targets.shape[0] * lax.axis_size("dp"),
        ),
        in_specs=[vmem()] * 18,
        out_specs=[vmem()] * 4,
        out_shape=[
            held((hidden, n), bf16),
            held((hidden, n), bf16),
            shape((half_rows, wide), f32),
            shape((half_rows, wide), bf16),
        ],
        scratch_shapes=[pltpu.VMEM((hidden, feature), f32), pltpu.VMEM((hidden, 128), f32)],
        compiler_params=params(20),
        cost_estimate=cost(4 * n * feature * hidden, MIB),
    )(
        *fields, left0, left1, right0, right1, far0, far1, target, scale_n, scale_v,
        *in_vmem(*acts, *slopes, *grid_latent, w_out_t),
    )

    swapped = lax.ppermute(send, "dp", [(0, 1), (1, 0)])

    grad_grid0, grad_grid1, rim_near, rim_far = pl.pallas_call(
        rim_kernel,
        in_specs=[vmem()] * 4,
        out_specs=[vmem()] * 4,
        out_shape=[held((feature, n), bf16)] * 2 + [shape((members, edge_rows, feature), bf16)] * 2,
        compiler_params=params(16),
        cost_estimate=cost(8 * n * feature * hidden, MIB),
    )(*in_vmem(grad_pre0, grad_pre1, halo_wt, w_in_t))

    quarter = half_rows // chips
    kept, *sends = pl.pallas_call(
        split_kernel,
        in_specs=[vmem(), vmem()],
        out_specs=[vmem()] * 4,
        out_shape=[shape((quarter, wide), f32)] + [shape((quarter, wide), bf16)] * 3,
        scratch_shapes=[pltpu.VMEM((chips, quarter, wide), f32)],
        compiler_params=params(8),
    )(keep, swapped)
    got = [along(s, d) for d, s in zip((1, 2, 3), sends)]

    got_near = lax.ppermute(rim_near, "space", first)
    got_far = lax.ppermute(rim_far, "space", second)

    middle = blocks // HALO - 2
    owned, edge = pl.pallas_call(
        owned_kernel,
        in_specs=[vmem()] * 3,
        out_specs=[hbm(), vmem()],
        out_shape=[
            shape((members, blocks * nodes, feature), f32),
            held((members, 2, edge_rows, feature), f32),
        ],
        scratch_shapes=[
            pltpu.VMEM((members * middle, edge_rows, feature), f32),
            pltpu.SemaphoreType.DMA((members * middle,)),
        ],
        compiler_params=params(20),
        cost_estimate=cost(2 * blocks * nodes * n * feature * members, 8 * MIB),
    )(*in_vmem(grad_grid0, grad_grid1, own_wt))

    last_rows = quarter // spaces
    spread = pl.pallas_call(
        scatter_kernel,
        in_specs=[vmem()] * 4 + [anywhere()],
        out_specs=vmem(),
        out_shape=shape((spaces, last_rows, wide), bf16),
        compiler_params=params(8),
    )(kept, *got, edge)
    spread = lax.all_to_all(spread, "space", 0, 0, tiled=True)
    grad_w_in, grad_w_out = pl.pallas_call(
        finish_kernel,
        in_specs=[vmem()],
        out_specs=[vmem()] * 2,
        out_shape=[shape((last_rows, feature), f32), shape((last_rows, variables), f32)],
        compiler_params=params(8),
    )(spread)

    grad_latent = pl.pallas_call(
        add_rim_kernel,
        in_specs=[hbm(), vmem(), vmem(), vmem()],
        out_specs=hbm(),
        out_shape=shape(owned.shape, f32),
        scratch_shapes=[
            pltpu.VMEM((2 * members, edge_rows, feature), f32),
            pltpu.SemaphoreType.DMA((2 * members,)),
        ],
        input_output_aliases={0: 0},
        compiler_params=params(8),
    )(owned, *in_vmem(edge), got_near, got_far)
    return grad_latent[None], grad_w_in, grad_w_out.T


def solution(mesh):
    placed = (
        P("dp", "member", "space", None),
        P("space", None, None, None),
        P("space", None),
        P("space"),
        P(),
        P(),
        P("dp", None, "space"),
        P("space"),
        P(),
    )
    return jax.shard_map(
        local,
        mesh=mesh,
        in_specs=placed,
        out_specs=(
            P("dp", "member", "space", None),
            P(("dp", "member", "space"), None),
            P(None, ("dp", "member", "space")),
        ),
        check_vma=False,
    )
```

```python
import functools

import jax
import jax.numpy as jnp
from jax import lax
from jax.experimental import pallas as pl
from jax.experimental.pallas import tpu as pltpu
from jax.sharding import PartitionSpec as P

HALO = 2
smooth_square = 0.1 * 0.1
gelu_scale = 0.7978845608028654
gelu_cubic = 0.044715
MIB = 1 << 20
f32 = jnp.float32
bf16 = jnp.bfloat16

NN = (((1,), (0,)), ((), ()))
NT = (((1,), (1,)), ((), ()))


def dot(a, b, dims=NN):
    return lax.dot_general(a, b, dims, preferred_element_type=f32)


def vmem():
    return pl.BlockSpec(memory_space=pltpu.VMEM)


def smem():
    return pl.BlockSpec(memory_space=pltpu.SMEM)


def hbm():
    return pl.BlockSpec(memory_space=pltpu.HBM)


def in_hbm(x):
    return pltpu.with_memory_space_constraint(x, pltpu.HBM)


def in_vmem(*xs):
    return [pltpu.with_memory_space_constraint(x, pltpu.VMEM) for x in xs]


def held(dims, dtype):
    return pltpu.VMEM(dims, dtype)


def anywhere():
    return pl.BlockSpec(memory_space=pl.ANY)


def cost(mega):
    return pl.CostEstimate(flops=mega * 1_000_000, bytes_accessed=mega * 4000, transcendentals=0)


def params(mib):
    return pltpu.CompilerParams(vmem_limit_bytes=mib * MIB)


def shape(dims, dtype):
    return jax.ShapeDtypeStruct(dims, dtype)


def rows_at(start, size):
    return pl.ds(pl.multiple_of(start * size, size), size)


def parity():
    return lax.rem(lax.axis_index("space"), 2)


def edges_kernel(lat, near0, far0, near1, far1, sems):
    step = near0.shape[0]
    last = lat.shape[1] - step
    odd = parity()
    top = pl.multiple_of((1 - odd) * last, step)
    bottom = pl.multiple_of(odd * last, step)
    copies = []
    for m, (near, far) in enumerate(((near0, far0), (near1, far1))):
        for out, start in ((near, top), (far, bottom)):
            copies.append(
                pltpu.make_async_copy(lat.at[m, pl.ds(start, step)], out, sems.at[len(copies)])
            )
            copies[-1].start()
    for copy in copies:
        copy.wait()


def halo_slot(e, blocks, spaces):
    at_space = lax.axis_index("space")
    odd = parity()
    below, above = e < HALO, e >= HALO + blocks
    outside = (below & (at_space > 0)) | (above & (at_space < spaces - 1))
    slot = jnp.where(below, e + (1 - odd) * HALO, e - HALO - blocks + odd * HALO)
    return outside, jnp.where(below | above, slot, 0)


def prepare_kernel(
    ids, count, lat_hbm, weight_hbm, w_in_hbm, w_out,
    acc0, acc1, halo_w, w_in_v, w_out_v, weight, lat, sems, *, spaces,
):
    tiles, slots, cells, nodes = weight.shape
    blocks = lat.shape[1]
    copies = [
        pltpu.make_async_copy(weight_hbm, weight, sems.at[0]),
        pltpu.make_async_copy(lat_hbm.at[0], lat.at[0], sems.at[1]),
        pltpu.make_async_copy(lat_hbm.at[1], lat.at[1], sems.at[2]),
        pltpu.make_async_copy(w_in_hbm, w_in_v, sems.at[3]),
    ]
    for c in copies:
        c.start()
    halo_w[...] = jnp.zeros_like(halo_w)
    w_out_v[...] = jnp.zeros_like(w_out_v)
    w_out_v[: w_out.shape[0]] = w_out[...]
    copies[0].wait()

    def place_tile(t, carry):
        for k in range(slots):
            e = ids[k, t]
            outside, slot = halo_slot(e, blocks, spaces)

            @pl.when((k < count[t]) & outside)
            def _():
                halo_w[rows_at(t, cells), rows_at(slot, nodes)] += weight[t, k]

        return carry

    lax.fori_loop(0, tiles, place_tile, 0)

    for m, acc in enumerate((acc0, acc1)):
        copies[1 + m].wait()
        for t in range(tiles):
            parts, at = [], []
            for k in range(slots):
                e = ids[k, t]
                mine = (k < count[t]) & (e >= HALO) & (e < HALO + blocks)
                w = weight[t, k]
                parts.append(jnp.where(mine, w, jnp.zeros_like(w)))
                at.append(jnp.clip(e - HALO, 0, blocks - 1))
            lhs = jnp.concatenate(parts, axis=1)
            rhs = jnp.concatenate([lat[m, a] for a in at], axis=0)
            acc[t * cells : (t + 1) * cells] = dot(lhs, rhs)
    copies[3].wait()


def turn_kernel(
    ids, count, weight, w_in, w_out, target, var_weight, later,
    halo_wt, own_wt, w_in_t, w_out_t, target_v, scale_v, square, *, spaces,
):
    tiles, slots, cells, nodes = weight.shape
    blocks = own_wt.shape[0] // nodes
    halo_wt[...] = jnp.zeros_like(halo_wt)
    own_wt[...] = jnp.zeros_like(own_wt)
    w_in_t[...] = w_in[...].T
    w_out_t[...] = w_out[...].T
    variables = target.shape[0]
    target_v[...] = jnp.zeros_like(target_v)
    target_v[:variables] = target[...]
    square[...] = jnp.zeros_like(square)
    square[:1, :variables] = var_weight[...]
    scale_v[...] = square[...].T[: scale_v.shape[0], :1]

    def place_tile(t, carry):
        for k in range(slots):
            e = ids[k, t]
            live = k < count[t]
            outside, slot = halo_slot(e, blocks, spaces)
            mine = (e >= HALO) & (e < HALO + blocks)
            block = jnp.clip(e - HALO, 0, blocks - 1)

            @pl.when(live & outside)
            def _():
                halo_wt[rows_at(slot, nodes), rows_at(t, cells)] += weight[t, k].T

            @pl.when(live & mine)
            def _():
                own_wt[rows_at(block, nodes), rows_at(t, cells)] += weight[t, k].T

        return carry

    lax.fori_loop(0, tiles, place_tile, 0)


def gelu_parts(x):
    square = x * x
    half = 0.5 + 0.5 * jnp.tanh(x * (gelu_scale + (gelu_scale * gelu_cubic) * square))
    return square, half


CHUNK = 256


def fields_kernel(acc, near, far, halo_w, w_in, w_out, later, lat_out, fields):
    count = acc.shape[0]
    half_k = near.shape[0]
    for start in range(0, count, 2 * CHUNK):
        at = slice(start, start + 2 * CHUNK)
        total = acc[at] + dot(halo_w[at, :half_k], near[...])
        total = total + dot(halo_w[at, half_k:], far[...])
        rounded = total.astype(bf16)
        lat_out[at] = rounded
        pre = dot(w_in[...], rounded, NT)
        _, half = gelu_parts(pre)
        fields[:, at] = dot(w_out[...], (pre * half).astype(bf16)).astype(bf16)


def slopes_kernel(lat, w_in, act_t, slope_t):
    count = lat.shape[0]
    for start in range(0, count, CHUNK):
        at = slice(start, start + CHUNK)
        x = dot(w_in[...], lat[at], NT)
        square, half = gelu_parts(x)
        act_t[:, at] = (x * half).astype(bf16)
        inner = x * (2.0 * gelu_scale + (6.0 * gelu_scale * gelu_cubic) * square)
        slope_t[:, at] = (half + half * (1.0 - half) * inner).astype(bf16)


def smooth_sign(u):
    return u * lax.rsqrt(u * u + smooth_square)


def spread_kernel(
    own0, own1, o10, o11, o20, o21, far0, target, part0, part1, *, ensemble,
):
    count = own0.shape[1]
    for start in range(0, count, CHUNK):
        at = slice(start, start + CHUNK)
        truth = target[:, at].astype(f32)
        mine = [own0[:, at].astype(f32), own1[:, at].astype(f32)]
        pair = smooth_sign(mine[0] - mine[1])
        spread = [pair, -pair]
        for other in (o10, o11, o20, o21, far0):
            theirs = other[:, at].astype(f32)
            for a in range(2):
                spread[a] = spread[a] + smooth_sign(mine[a] - theirs)
        for a, part in enumerate((part0, part1)):
            value = smooth_sign(mine[a] - truth) * (1.0 / ensemble)
            part[:, at] = value - spread[a] * (1.0 / (ensemble * (ensemble - 1)))


def weights_kernel(
    own0, own1, far1, part0, part1, area, var_weight,
    act0, act1, slope0, slope1, lat0, lat1, w_out_t,
    grad_pre0, grad_pre1, keep, send, total_in, total_out, *, ensemble, states,
):
    count = own0.shape[1]
    for start in range(0, count, CHUNK):
        at = slice(start, start + CHUNK)
        mine = [own0[:, at].astype(f32), own1[:, at].astype(f32)]
        theirs = far1[:, at].astype(f32)
        cell_weight = area[:, at] * var_weight[...] * (1.0 / states)
        cots = []
        for a, part in enumerate((part0, part1)):
            spread = smooth_sign(mine[a] - theirs)
            value = part[:, at] - spread * (1.0 / (ensemble * (ensemble - 1)))
            cots.append((cell_weight * value).astype(bf16))
        cot = jnp.concatenate(cots, axis=1)
        grad_act = dot(w_out_t[...], cot)
        slope = jnp.concatenate([slope0[:, at], slope1[:, at]], axis=1)
        pre = (grad_act * slope.astype(f32)).astype(bf16)
        grad_pre0[:, at] = pre[:, :CHUNK]
        grad_pre1[:, at] = pre[:, CHUNK:]
        part_in = dot(pre, jnp.concatenate([lat0[at], lat1[at]], axis=0))
        act = jnp.concatenate([act0[:, at], act1[:, at]], axis=1)
        part_out = dot(act, cot, NT)
        if start == 0:
            total_in[...] = part_in
            total_out[...] = jnp.zeros_like(total_out)
            total_out[:, : part_out.shape[1]] = part_out
        else:
            total_in[...] += part_in
            total_out[:, : part_out.shape[1]] += part_out
    rows = keep.shape[0]
    wide = total_in.shape[1]
    here = lax.axis_index("dp")
    stay, leave = rows_at(here, rows), rows_at(1 - here, rows)
    keep[:, :wide] = total_in[stay]
    keep[:, wide:] = total_out[stay]
    send[:, :wide] = total_in[leave].astype(bf16)
    send[:, wide:] = total_out[leave].astype(bf16)


def rim_kernel(grad_pre0, grad_pre1, halo_wt, w_in_t, grad_grid0, grad_grid1, near, far):
    half_k = near.shape[1]
    for m, (grad_pre, grad_grid) in enumerate(
        ((grad_pre0, grad_grid0), (grad_pre1, grad_grid1))
    ):
        grad_grid[...] = dot(w_in_t[...], grad_pre[...]).astype(bf16)
        near[m] = dot(halo_wt[:half_k], grad_grid[...], NT).astype(bf16)
        far[m] = dot(halo_wt[half_k:], grad_grid[...], NT).astype(bf16)


def owned_kernel(grad_grid0, grad_grid1, own_wt, later, out, edge, parts, sems):
    step = edge.shape[2]
    count = own_wt.shape[0] // step
    copies = []
    for m, grad_grid in enumerate((grad_grid0, grad_grid1)):
        for i in range(count):
            value = dot(own_wt[i * step : (i + 1) * step], grad_grid[...], NT)
            if i == 0:
                edge[m, 0] = value
            elif i == count - 1:
                edge[m, 1] = value
            else:
                slot = len(copies)
                parts[slot] = value
                copy = pltpu.make_async_copy(
                    parts.at[slot], out.at[m, i * step : (i + 1) * step], sems.at[slot]
                )
                copy.start()
                copies.append(copy)
    for copy in copies:
        copy.wait()


def add_rim_kernel(base, edge, near, far, out, parts, sems):
    step = edge.shape[2]
    last = out.shape[1] - step
    odd = parity()
    copies = []
    for side, got in ((1 - odd, near), (odd, far)):
        start = pl.multiple_of(side * last, step)
        for m in range(edge.shape[0]):
            slot = len(copies)
            parts[slot] = edge[m, side] + got[m].astype(f32)
            copy = pltpu.make_async_copy(
                parts.at[slot], out.at[m, pl.ds(start, step)], sems.at[slot]
            )
            copy.start()
            copies.append(copy)
    for copy in copies:
        copy.wait()


def halve_kernel(kept, got, keep, send, total, *, bit):
    rows = keep.shape[0]
    total[...] = kept[...] + got[...].astype(f32)
    here = lax.rem(lax.axis_index("member") // bit, 2)
    keep[...] = total[rows_at(here, rows)]
    send[...] = total[rows_at(1 - here, rows)].astype(send.dtype)


def halve(kept, got, bit):
    rows, wide = kept.shape[0] // 2, kept.shape[1]
    return pl.pallas_call(
        functools.partial(halve_kernel, bit=bit),
        in_specs=[vmem()] * 2,
        out_specs=[vmem()] * 2,
        out_shape=[shape((rows, wide), f32), shape((rows, wide), bf16)],
        scratch_shapes=[pltpu.VMEM(kept.shape, f32)],
        compiler_params=params(8),
        cost_estimate=cost(2000),
    )(kept, got)


def scatter_kernel(kept, got, later, out):
    value = kept[...] + got[...].astype(f32)
    parts, rows = out.shape[0], out.shape[1]
    for p in range(parts):
        out[p] = value[p * rows : (p + 1) * rows].astype(out.dtype)


def finish_kernel(got, grad_in, grad_out):
    value = got[0].astype(f32)
    for p in range(1, got.shape[0]):
        value = value + got[p].astype(f32)
    wide = grad_in.shape[1]
    grad_in[...] = value[:, :wide]
    grad_out[...] = value[:, wide : wide + grad_out.shape[1]]


def ring(count, distance):
    return [(i, (i + distance) % count) for i in range(count)]


def local(latents, edge_weight, block_ids, block_count, w_in, w_out, targets, area, var_weight):
    members = latents.shape[1]
    feature = latents.shape[3]
    hidden = w_in.shape[0]
    variables = w_out.shape[0]
    rows_v = (variables + 7) // 8 * 8
    tiles, slots, cells, nodes = edge_weight.shape
    n = tiles * cells
    lat = latents[0].reshape(members, -1, nodes, feature)
    blocks = lat.shape[1]
    edge_rows = HALO * nodes
    rim_rows = 2 * edge_rows
    spaces = lax.axis_size("space")
    chips = lax.axis_size("member")
    ids = block_ids.T
    first = [(i, i ^ 1) for i in range(spaces)]
    second = [(i, ((i + 1) ^ 1) - 1) for i in range(spaces)]
    second = [(i, j % spaces) for i, j in second]

    edges = pl.pallas_call(
        edges_kernel,
        in_specs=[hbm()],
        out_specs=[vmem()] * 4,
        out_shape=[shape((edge_rows, feature), bf16)] * 4,
        scratch_shapes=[pltpu.SemaphoreType.DMA((4,))],
        compiler_params=params(8),
    )(in_hbm(latents[0]))
    halos = []
    for m in range(members):
        near = lax.ppermute(edges[2 * m], "space", first)
        far = lax.ppermute(edges[2 * m + 1], "space", second)
        halos.append((near, far))

    scale_n = area[None, :]

    acc0, acc1, halo_w, w_in_v, w_out_v, weight_v = pl.pallas_call(
        functools.partial(prepare_kernel, spaces=spaces),
        in_specs=[smem(), smem(), hbm(), hbm(), hbm(), vmem()],
        out_specs=[vmem()] * 6,
        out_shape=[
            held((n, feature), f32),
            held((n, feature), f32),
            held((n, rim_rows), bf16),
            held((hidden, feature), bf16),
            held((rows_v, hidden), bf16),
            held(edge_weight.shape, bf16),
        ],
        scratch_shapes=[
            pltpu.VMEM(lat.shape, bf16),
            pltpu.SemaphoreType.DMA((4,)),
        ],
        compiler_params=params(12),
        cost_estimate=cost(2000),
    )(ids, block_count, in_hbm(lat), in_hbm(edge_weight), in_hbm(w_in), in_hbm(w_out))

    def along(x, distance):
        return lax.ppermute(x, "member", ring(chips, distance))

    grid_latent, fields, acts, slopes = [], [], [], []
    for m, acc in enumerate((acc0, acc1)):
        near, far = halos[m]
        lat_m, fields_m = pl.pallas_call(
            fields_kernel,
            in_specs=[vmem()] * 6 + [anywhere()],
            out_specs=[vmem()] * 2,
            out_shape=[held((n, feature), bf16), shape((rows_v, n), bf16)],
            compiler_params=params(8),
            cost_estimate=cost(100),
        )(*in_vmem(acc), near, far, *in_vmem(halo_w, w_in_v, w_out_v), slopes[-1] if slopes else halo_w)
        grid_latent.append(lat_m)
        fields.append(fields_m)
        if m == 0:
            left0 = along(fields_m, 1)
            right0 = along(fields_m, -1)
        else:
            lat_m, left0, right0 = lax.optimization_barrier((lat_m, left0, right0))
        act_m, slope_m = pl.pallas_call(
            slopes_kernel,
            in_specs=[vmem()] * 2,
            out_specs=[vmem()] * 2,
            out_shape=[held((hidden, n), bf16)] * 2,
            compiler_params=params(8),
            cost_estimate=cost(100),
        )(*in_vmem(lat_m, w_in_v))
        acts.append(act_m)
        slopes.append(slope_m)

    halo_wt, own_wt, w_in_t, w_out_t, target, scale_v = pl.pallas_call(
        functools.partial(turn_kernel, spaces=spaces),
        in_specs=[smem(), smem()] + [vmem()] * 5 + [anywhere()],
        out_specs=[vmem()] * 6,
        out_shape=[
            held((rim_rows, n), bf16),
            held((blocks * nodes, n), bf16),
            held((feature, hidden), bf16),
            held((hidden, rows_v), bf16),
            held((rows_v, n), bf16),
            held((rows_v, 1), f32),
        ],
        scratch_shapes=[pltpu.VMEM((128, 128), f32)],
        compiler_params=params(8),
        cost_estimate=cost(100),
    )(
        ids, block_count, *in_vmem(weight_v, w_in_v, w_out_v), targets[0], var_weight[None],
        slopes[1],
    )

    right1 = along(fields[1], -1)
    left1 = along(fields[1], 1)
    far0 = along(left0, 1)
    held_right1, _ = lax.optimization_barrier((right1, slopes[1]))
    far1 = along(held_right1, -1)

    part0, part1 = pl.pallas_call(
        functools.partial(spread_kernel, ensemble=members * chips),
        in_specs=[vmem()] * 8,
        out_specs=[vmem()] * 2,
        out_shape=[held((rows_v, n), f32)] * 2,
        compiler_params=params(8),
        cost_estimate=cost(100),
    )(*fields, left0, left1, right0, right1, far0, *in_vmem(target))

    wide = feature + 128
    half_rows = hidden // 2
    grad_pre0, grad_pre1, keep, send = pl.pallas_call(
        functools.partial(
            weights_kernel,
            ensemble=members * chips,
            states=targets.shape[0] * lax.axis_size("dp"),
        ),
        in_specs=[vmem()] * 14,
        out_specs=[vmem()] * 4,
        out_shape=[
            held((hidden, n), bf16),
            held((hidden, n), bf16),
            shape((half_rows, wide), f32),
            shape((half_rows, wide), bf16),
        ],
        scratch_shapes=[pltpu.VMEM((hidden, feature), f32), pltpu.VMEM((hidden, 128), f32)],
        compiler_params=params(12),
        cost_estimate=cost(2000),
    )(
        *fields, far1, *in_vmem(part0, part1), scale_n, *in_vmem(scale_v),
        *in_vmem(*acts, *slopes, *grid_latent, w_out_t),
    )

    swapped = lax.ppermute(send, "dp", [(0, 1), (1, 0)])

    grad_grid0, grad_grid1, rim_near, rim_far = pl.pallas_call(
        rim_kernel,
        in_specs=[vmem()] * 4,
        out_specs=[vmem()] * 4,
        out_shape=[held((feature, n), bf16)] * 2 + [shape((members, edge_rows, feature), bf16)] * 2,
        compiler_params=params(8),
        cost_estimate=cost(2000),
    )(*in_vmem(grad_pre0, grad_pre1, halo_wt, w_in_t))

    quarter = half_rows // chips
    swapped, _ = lax.optimization_barrier((swapped, grad_grid0))
    kept, send = halve(keep, swapped, 2)
    got = lax.ppermute(send, "member", [(i, chips - 1 - i) for i in range(chips)])
    rim_near, rim_far, _ = lax.optimization_barrier((rim_near, rim_far, send))
    got_near = lax.ppermute(rim_near, "space", first)
    got_far = lax.ppermute(rim_far, "space", second)
    kept, send = halve(kept, got, 1)
    got = lax.ppermute(send, "member", [(i, i ^ 1) for i in range(chips)])

    middle = blocks // HALO - 2
    owned, edge = pl.pallas_call(
        owned_kernel,
        in_specs=[vmem()] * 3 + [anywhere()],
        out_specs=[hbm(), vmem()],
        out_shape=[
            shape((members, blocks * nodes, feature), f32),
            held((members, 2, edge_rows, feature), f32),
        ],
        scratch_shapes=[
            pltpu.VMEM((members * middle, edge_rows, feature), f32),
            pltpu.SemaphoreType.DMA((members * middle,)),
        ],
        compiler_params=params(12),
        cost_estimate=cost(2000),
    )(*in_vmem(grad_grid0, grad_grid1, own_wt), send)

    last_rows = quarter // spaces
    spread = pl.pallas_call(
        scatter_kernel,
        in_specs=[vmem()] * 2 + [anywhere()],
        out_specs=vmem(),
        out_shape=shape((spaces, last_rows, wide), bf16),
        compiler_params=params(8),
    )(kept, got, edge)
    spread = lax.all_to_all(spread, "space", 0, 0, tiled=True)
    grad_w_in, grad_w_out = pl.pallas_call(
        finish_kernel,
        in_specs=[vmem()],
        out_specs=[vmem()] * 2,
        out_shape=[shape((last_rows, feature), f32), shape((last_rows, variables), f32)],
        compiler_params=params(8),
    )(spread)

    grad_latent = pl.pallas_call(
        add_rim_kernel,
        in_specs=[hbm(), vmem(), vmem(), vmem()],
        out_specs=hbm(),
        out_shape=shape(owned.shape, f32),
        scratch_shapes=[
            pltpu.VMEM((2 * members, edge_rows, feature), f32),
            pltpu.SemaphoreType.DMA((2 * members,)),
        ],
        input_output_aliases={0: 0},
        compiler_params=params(8),
    )(owned, *in_vmem(edge), got_near, got_far)
    return grad_latent[None], grad_w_in, grad_w_out.T


def solution(mesh):
    placed = (
        P("dp", "member", "space", None),
        P("space", None, None, None),
        P("space", None),
        P("space"),
        P(),
        P(),
        P("dp", None, "space"),
        P("space"),
        P(),
    )
    return jax.shard_map(
        local,
        mesh=mesh,
        in_specs=placed,
        out_specs=(
            P("dp", "member", "space", None),
            P(("dp", "member", "space"), None),
            P(None, ("dp", "member", "space")),
        ),
        check_vma=False,
    )
```

```python
import functools

import jax
import jax.numpy as jnp
from jax import lax
from jax.experimental import pallas as pl
from jax.experimental.pallas import tpu as pltpu
from jax.sharding import PartitionSpec as P

HALO = 2
smooth_square = 0.1 * 0.1
gelu_scale = 0.7978845608028654
gelu_cubic = 0.044715
MIB = 1 << 20
f32 = jnp.float32
bf16 = jnp.bfloat16

NN = (((1,), (0,)), ((), ()))
NT = (((1,), (1,)), ((), ()))


def dot(a, b, dims=NN):
    return lax.dot_general(a, b, dims, preferred_element_type=f32)


def vmem():
    return pl.BlockSpec(memory_space=pltpu.VMEM)


def smem():
    return pl.BlockSpec(memory_space=pltpu.SMEM)


def hbm():
    return pl.BlockSpec(memory_space=pltpu.HBM)


def in_hbm(x):
    return pltpu.with_memory_space_constraint(x, pltpu.HBM)


def in_vmem(*xs):
    return [pltpu.with_memory_space_constraint(x, pltpu.VMEM) for x in xs]


def held(dims, dtype):
    return pltpu.VMEM(dims, dtype)


def anywhere():
    return pl.BlockSpec(memory_space=pl.ANY)


def cost(mega):
    return pl.CostEstimate(flops=mega * 1_000_000, bytes_accessed=mega * 4000, transcendentals=0)


def params(mib):
    return pltpu.CompilerParams(vmem_limit_bytes=mib * MIB)


def shape(dims, dtype):
    return jax.ShapeDtypeStruct(dims, dtype)


def rows_at(start, size):
    return pl.ds(pl.multiple_of(start * size, size), size)


def parity():
    return lax.rem(lax.axis_index("space") + 1, 2)


def edges_kernel(lat, near0, far0, near1, far1, sems):
    step = near0.shape[0]
    last = lat.shape[1] - step
    odd = parity()
    top = pl.multiple_of((1 - odd) * last, step)
    bottom = pl.multiple_of(odd * last, step)
    copies = []
    for m, (near, far) in enumerate(((near0, far0), (near1, far1))):
        for out, start in ((near, top), (far, bottom)):
            copies.append(
                pltpu.make_async_copy(lat.at[m, pl.ds(start, step)], out, sems.at[len(copies)])
            )
            copies[-1].start()
    for copy in copies:
        copy.wait()


def halo_slot(e, blocks, spaces):
    at_space = lax.axis_index("space")
    odd = parity()
    below, above = e < HALO, e >= HALO + blocks
    outside = (below & (at_space > 0)) | (above & (at_space < spaces - 1))
    slot = jnp.where(below, e + (1 - odd) * HALO, e - HALO - blocks + odd * HALO)
    return outside, jnp.where(below | above, slot, 0)


def prepare_kernel(
    ids, count, lat_hbm, weight_hbm, w_in_hbm, w_out,
    acc0, acc1, halo_w, w_in_v, w_out_v, weight, lat, sems, *, spaces,
):
    tiles, slots, cells, nodes = weight.shape
    blocks = lat.shape[1]
    copies = [
        pltpu.make_async_copy(weight_hbm, weight, sems.at[0]),
        pltpu.make_async_copy(lat_hbm.at[0], lat.at[0], sems.at[1]),
        pltpu.make_async_copy(lat_hbm.at[1], lat.at[1], sems.at[2]),
        pltpu.make_async_copy(w_in_hbm, w_in_v, sems.at[3]),
    ]
    for c in copies:
        c.start()
    halo_w[...] = jnp.zeros_like(halo_w)
    w_out_v[...] = jnp.zeros_like(w_out_v)
    w_out_v[: w_out.shape[0]] = w_out[...]
    copies[0].wait()

    def place_tile(t, carry):
        for k in range(slots):
            e = ids[k, t]
            outside, slot = halo_slot(e, blocks, spaces)

            @pl.when((k < count[t]) & outside)
            def _():
                halo_w[rows_at(t, cells), rows_at(slot, nodes)] += weight[t, k]

        return carry

    lax.fori_loop(0, tiles, place_tile, 0)

    for m, acc in enumerate((acc0, acc1)):
        copies[1 + m].wait()
        for t in range(tiles):
            parts, at = [], []
            for k in range(slots):
                e = ids[k, t]
                mine = (k < count[t]) & (e >= HALO) & (e < HALO + blocks)
                w = weight[t, k]
                parts.append(jnp.where(mine, w, jnp.zeros_like(w)))
                at.append(jnp.clip(e - HALO, 0, blocks - 1))
            lhs = jnp.concatenate(parts, axis=1)
            rhs = jnp.concatenate([lat[m, a] for a in at], axis=0)
            acc[t * cells : (t + 1) * cells] = dot(lhs, rhs)
    copies[3].wait()


def turn_kernel(
    ids, count, weight, w_in, w_out, target, var_weight, later,
    halo_wt, own_wt, w_in_t, w_out_t, target_v, scale_v, square, *, spaces,
):
    tiles, slots, cells, nodes = weight.shape
    blocks = own_wt.shape[0] // nodes
    halo_wt[...] = jnp.zeros_like(halo_wt)
    own_wt[...] = jnp.zeros_like(own_wt)
    w_in_t[...] = w_in[...].T
    w_out_t[...] = w_out[...].T
    variables = target.shape[0]
    target_v[...] = jnp.zeros_like(target_v)
    target_v[:variables] = target[...]
    square[...] = jnp.zeros_like(square)
    square[:1, :variables] = var_weight[...]
    scale_v[...] = square[...].T[: scale_v.shape[0], :1]

    def place_tile(t, carry):
        for k in range(slots):
            e = ids[k, t]
            live = k < count[t]
            outside, slot = halo_slot(e, blocks, spaces)
            mine = (e >= HALO) & (e < HALO + blocks)
            block = jnp.clip(e - HALO, 0, blocks - 1)

            @pl.when(live & outside)
            def _():
                halo_wt[rows_at(slot, nodes), rows_at(t, cells)] += weight[t, k].T

            @pl.when(live & mine)
            def _():
                own_wt[rows_at(block, nodes), rows_at(t, cells)] += weight[t, k].T

        return carry

    lax.fori_loop(0, tiles, place_tile, 0)


def gelu_parts(x):
    square = x * x
    half = 0.5 + 0.5 * jnp.tanh(x * (gelu_scale + (gelu_scale * gelu_cubic) * square))
    return square, half


CHUNK = 256


def fields_kernel(acc, near, far, halo_w, w_in, w_out, lat_out, fields):
    count = acc.shape[0]
    half_k = near.shape[0]
    for start in range(0, count, 2 * CHUNK):
        at = slice(start, start + 2 * CHUNK)
        total = acc[at] + dot(halo_w[at, :half_k], near[...])
        total = total + dot(halo_w[at, half_k:], far[...])
        rounded = total.astype(bf16)
        lat_out[at] = rounded
        pre = dot(w_in[...], rounded, NT)
        _, half = gelu_parts(pre)
        fields[:, at] = dot(w_out[...], (pre * half).astype(bf16)).astype(bf16)


def slopes_kernel(lat, w_in, act_t, slope_t):
    count = lat.shape[0]
    for start in range(0, count, CHUNK):
        at = slice(start, start + CHUNK)
        x = dot(w_in[...], lat[at], NT)
        square, half = gelu_parts(x)
        act_t[:, at] = (x * half).astype(bf16)
        inner = x * (2.0 * gelu_scale + (6.0 * gelu_scale * gelu_cubic) * square)
        slope_t[:, at] = (half + half * (1.0 - half) * inner).astype(bf16)


def smooth_sign(u):
    return u * lax.rsqrt(u * u + smooth_square)


def spread_kernel(
    own0, own1, o10, o11, o20, o21, far0, target, part0, part1, *, ensemble,
):
    count = own0.shape[1]
    for start in range(0, count, CHUNK):
        at = slice(start, start + CHUNK)
        truth = target[:, at].astype(f32)
        mine = [own0[:, at].astype(f32), own1[:, at].astype(f32)]
        pair = smooth_sign(mine[0] - mine[1])
        spread = [pair, -pair]
        for other in (o10, o11, o20, o21, far0):
            theirs = other[:, at].astype(f32)
            for a in range(2):
                spread[a] = spread[a] + smooth_sign(mine[a] - theirs)
        for a, part in enumerate((part0, part1)):
            value = smooth_sign(mine[a] - truth) * (1.0 / ensemble)
            part[:, at] = value - spread[a] * (1.0 / (ensemble * (ensemble - 1)))


def weights_kernel(
    own0, own1, far1, part0, part1, area, var_weight,
    act0, act1, slope0, slope1, lat0, lat1, w_out_t,
    grad_pre0, grad_pre1, keep, send, total_in, total_out, *, ensemble, states,
):
    count = own0.shape[1]
    for start in range(0, count, CHUNK):
        at = slice(start, start + CHUNK)
        mine = [own0[:, at].astype(f32), own1[:, at].astype(f32)]
        theirs = far1[:, at].astype(f32)
        cell_weight = area[:, at] * var_weight[...] * (1.0 / states)
        cots = []
        for a, part in enumerate((part0, part1)):
            spread = smooth_sign(mine[a] - theirs)
            value = part[:, at] - spread * (1.0 / (ensemble * (ensemble - 1)))
            cots.append((cell_weight * value).astype(bf16))
        cot = jnp.concatenate(cots, axis=1)
        grad_act = dot(w_out_t[...], cot)
        slope = jnp.concatenate([slope0[:, at], slope1[:, at]], axis=1)
        pre = (grad_act * slope.astype(f32)).astype(bf16)
        grad_pre0[:, at] = pre[:, :CHUNK]
        grad_pre1[:, at] = pre[:, CHUNK:]
        part_in = dot(pre, jnp.concatenate([lat0[at], lat1[at]], axis=0))
        act = jnp.concatenate([act0[:, at], act1[:, at]], axis=1)
        part_out = dot(act, cot, NT)
        if start == 0:
            total_in[...] = part_in
            total_out[...] = jnp.zeros_like(total_out)
            total_out[:, : part_out.shape[1]] = part_out
        else:
            total_in[...] += part_in
            total_out[:, : part_out.shape[1]] += part_out
    rows = keep.shape[0]
    wide = total_in.shape[1]
    here = lax.axis_index("dp")
    stay, leave = rows_at(here, rows), rows_at(1 - here, rows)
    keep[:, :wide] = total_in[stay]
    keep[:, wide:] = total_out[stay]
    send[:, :wide] = total_in[leave].astype(bf16)
    send[:, wide:] = total_out[leave].astype(bf16)


def rim_kernel(grad_pre0, grad_pre1, halo_wt, w_in_t, grad_grid0, grad_grid1, near, far):
    half_k = near.shape[1]
    for m, (grad_pre, grad_grid) in enumerate(
        ((grad_pre0, grad_grid0), (grad_pre1, grad_grid1))
    ):
        grad_grid[...] = dot(w_in_t[...], grad_pre[...]).astype(bf16)
        near[m] = dot(halo_wt[:half_k], grad_grid[...], NT).astype(bf16)
        far[m] = dot(halo_wt[half_k:], grad_grid[...], NT).astype(bf16)


def owned_kernel(grad_grid, own_wt, base, out, edge, parts, sems, *, member):
    step = edge.shape[1]
    count = own_wt.shape[0] // step
    copies = []
    for i in range(count):
        value = dot(own_wt[i * step : (i + 1) * step], grad_grid[...], NT)
        if i == 0:
            edge[0] = value
        elif i == count - 1:
            edge[1] = value
        else:
            slot = len(copies)
            parts[slot] = value
            copy = pltpu.make_async_copy(
                parts.at[slot], out.at[member, i * step : (i + 1) * step], sems.at[slot]
            )
            copy.start()
            copies.append(copy)
    for copy in copies:
        copy.wait()


def finish_kernel(
    base, edge0, edge1, near, far, got, out, grad_in, grad_out, parts, sems,
):
    step = edge0.shape[1]
    last = out.shape[1] - step
    odd = parity()
    copies = []
    for side, rim in ((1 - odd, near), (odd, far)):
        start = pl.multiple_of(side * last, step)
        for m, edge in enumerate((edge0, edge1)):
            slot = len(copies)
            parts[slot] = edge[side] + rim[m].astype(f32)
            copy = pltpu.make_async_copy(
                parts.at[slot], out.at[m, pl.ds(start, step)], sems.at[slot]
            )
            copy.start()
            copies.append(copy)
    value = got[0].astype(f32)
    for p in range(1, got.shape[0]):
        value = value + got[p].astype(f32)
    wide = grad_in.shape[1]
    grad_in[...] = value[:, :wide]
    grad_out[...] = value[:, wide : wide + grad_out.shape[1]]
    for copy in copies:
        copy.wait()


def halve_kernel(kept, got, keep, send, total, *, bit):
    rows = keep.shape[0]
    total[...] = kept[...] + got[...].astype(f32)
    here = lax.rem(lax.axis_index("member") // bit, 2)
    keep[...] = total[rows_at(here, rows)]
    send[...] = total[rows_at(1 - here, rows)].astype(send.dtype)


def halve(kept, got, bit):
    rows, wide = kept.shape[0] // 2, kept.shape[1]
    return pl.pallas_call(
        functools.partial(halve_kernel, bit=bit),
        in_specs=[vmem()] * 2,
        out_specs=[vmem()] * 2,
        out_shape=[shape((rows, wide), f32), shape((rows, wide), bf16)],
        scratch_shapes=[pltpu.VMEM(kept.shape, f32)],
        compiler_params=params(8),
        cost_estimate=cost(2000),
    )(kept, got)


def scatter_kernel(kept, got, out):
    value = kept[...] + got[...].astype(f32)
    parts, rows = out.shape[0], out.shape[1]
    for p in range(parts):
        out[p] = value[p * rows : (p + 1) * rows].astype(out.dtype)


def ring(count, distance):
    return [(i, (i + distance) % count) for i in range(count)]


def local(latents, edge_weight, block_ids, block_count, w_in, w_out, targets, area, var_weight):
    members = latents.shape[1]
    feature = latents.shape[3]
    hidden = w_in.shape[0]
    variables = w_out.shape[0]
    rows_v = (variables + 7) // 8 * 8
    tiles, slots, cells, nodes = edge_weight.shape
    n = tiles * cells
    lat = latents[0].reshape(members, -1, nodes, feature)
    blocks = lat.shape[1]
    edge_rows = HALO * nodes
    rim_rows = 2 * edge_rows
    spaces = lax.axis_size("space")
    chips = lax.axis_size("member")
    ids = block_ids.T
    first = [(i, (((i + 1) ^ 1) - 1) % spaces) for i in range(spaces)]
    second = [(i, i ^ 1) for i in range(spaces)]

    edges = pl.pallas_call(
        edges_kernel,
        in_specs=[hbm()],
        out_specs=[vmem()] * 4,
        out_shape=[shape((edge_rows, feature), bf16)] * 4,
        scratch_shapes=[pltpu.SemaphoreType.DMA((4,))],
        compiler_params=params(8),
    )(in_hbm(latents[0]))
    halos = []
    for m in range(members):
        far = lax.ppermute(edges[2 * m + 1], "space", second)
        near = lax.ppermute(edges[2 * m], "space", first)
        halos.append((near, far))

    scale_n = area[None, :]

    acc0, acc1, halo_w, w_in_v, w_out_v, weight_v = pl.pallas_call(
        functools.partial(prepare_kernel, spaces=spaces),
        in_specs=[smem(), smem(), hbm(), hbm(), hbm(), vmem()],
        out_specs=[vmem()] * 6,
        out_shape=[
            held((n, feature), f32),
            held((n, feature), f32),
            held((n, rim_rows), bf16),
            held((hidden, feature), bf16),
            held((rows_v, hidden), bf16),
            held(edge_weight.shape, bf16),
        ],
        scratch_shapes=[
            pltpu.VMEM(lat.shape, bf16),
            pltpu.SemaphoreType.DMA((4,)),
        ],
        compiler_params=params(12),
        cost_estimate=cost(2000),
    )(ids, block_count, in_hbm(lat), in_hbm(edge_weight), in_hbm(w_in), in_hbm(w_out))

    def along(x, distance):
        return lax.ppermute(x, "member", ring(chips, distance))

    def fields_of(acc, near, far):
        return pl.pallas_call(
            fields_kernel,
            in_specs=[vmem()] * 6,
            out_specs=[vmem()] * 2,
            out_shape=[held((n, feature), bf16), shape((rows_v, n), bf16)],
            compiler_params=params(8),
            cost_estimate=cost(100),
        )(*in_vmem(acc), near, far, *in_vmem(halo_w, w_in_v, w_out_v))

    def slopes_of(lat_m):
        return pl.pallas_call(
            slopes_kernel,
            in_specs=[vmem()] * 2,
            out_specs=[vmem()] * 2,
            out_shape=[held((hidden, n), bf16)] * 2,
            compiler_params=params(8),
            cost_estimate=cost(100),
        )(*in_vmem(lat_m, w_in_v))

    lat0, fields0 = fields_of(acc0, *halos[0])
    left0 = along(fields0, 1)
    right0 = along(fields0, -1)
    lat1, fields1 = fields_of(acc1, *halos[1])
    right1 = along(fields1, -1)
    left1 = along(fields1, 1)
    fields = [fields0, fields1]
    first_lat, left0, right0 = lax.optimization_barrier((lat0, left0, right0))
    act0, slope0 = slopes_of(first_lat)
    far0 = along(left0, 1)
    second_lat, _ = lax.optimization_barrier((lat1, slope0))
    act1, slope1 = slopes_of(second_lat)
    held_right1, _ = lax.optimization_barrier((right1, slope1))
    far1 = along(held_right1, -1)
    grid_latent, acts, slopes = [lat0, lat1], [act0, act1], [slope0, slope1]

    halo_wt, own_wt, w_in_t, w_out_t, target, scale_v = pl.pallas_call(
        functools.partial(turn_kernel, spaces=spaces),
        in_specs=[smem(), smem()] + [vmem()] * 5 + [anywhere()],
        out_specs=[vmem()] * 6,
        out_shape=[
            held((rim_rows, n), bf16),
            held((blocks * nodes, n), bf16),
            held((feature, hidden), bf16),
            held((hidden, rows_v), bf16),
            held((rows_v, n), bf16),
            held((rows_v, 1), f32),
        ],
        scratch_shapes=[pltpu.VMEM((128, 128), f32)],
        compiler_params=params(8),
        cost_estimate=cost(100),
    )(
        ids, block_count, *in_vmem(weight_v, w_in_v, w_out_v), targets[0], var_weight[None],
        slopes[1],
    )

    part0, part1 = pl.pallas_call(
        functools.partial(spread_kernel, ensemble=members * chips),
        in_specs=[vmem()] * 8,
        out_specs=[vmem()] * 2,
        out_shape=[held((rows_v, n), f32)] * 2,
        compiler_params=params(8),
        cost_estimate=cost(100),
    )(*fields, left0, left1, right0, right1, far0, *in_vmem(target))

    wide = feature + 128
    half_rows = hidden // 2
    grad_pre0, grad_pre1, keep, send = pl.pallas_call(
        functools.partial(
            weights_kernel,
            ensemble=members * chips,
            states=targets.shape[0] * lax.axis_size("dp"),
        ),
        in_specs=[vmem()] * 14,
        out_specs=[vmem()] * 4,
        out_shape=[
            held((hidden, n), bf16),
            held((hidden, n), bf16),
            shape((half_rows, wide), f32),
            shape((half_rows, wide), bf16),
        ],
        scratch_shapes=[pltpu.VMEM((hidden, feature), f32), pltpu.VMEM((hidden, 128), f32)],
        compiler_params=params(12),
        cost_estimate=cost(2000),
    )(
        *fields, far1, *in_vmem(part0, part1), scale_n, *in_vmem(scale_v),
        *in_vmem(*acts, *slopes, *grid_latent, w_out_t),
    )

    swapped = lax.ppermute(send, "dp", [(0, 1), (1, 0)])

    grad_grid0, grad_grid1, rim_near, rim_far = pl.pallas_call(
        rim_kernel,
        in_specs=[vmem()] * 4,
        out_specs=[vmem()] * 4,
        out_shape=[held((feature, n), bf16)] * 2 + [shape((members, edge_rows, feature), bf16)] * 2,
        compiler_params=params(8),
        cost_estimate=cost(2000),
    )(*in_vmem(grad_pre0, grad_pre1, halo_wt, w_in_t))

    quarter = half_rows // chips
    middle = blocks // HALO - 2

    def owned_of(member, grad_grid, base):
        whole = shape((members, blocks * nodes, feature), f32)
        aliased = {} if base is None else {2: 0}
        base = grad_grid if base is None else base
        return pl.pallas_call(
            functools.partial(owned_kernel, member=member),
            in_specs=[vmem()] * 2 + [anywhere()],
            out_specs=[hbm(), vmem()],
            out_shape=[whole, held((2, edge_rows, feature), f32)],
            scratch_shapes=[
                pltpu.VMEM((middle, edge_rows, feature), f32),
                pltpu.SemaphoreType.DMA((middle,)),
            ],
            input_output_aliases=aliased,
            compiler_params=params(8),
            cost_estimate=cost(2000),
        )(*in_vmem(grad_grid, own_wt), base)

    swapped, _ = lax.optimization_barrier((swapped, grad_grid0))
    kept, send = halve(keep, swapped, 2)
    got = lax.ppermute(send, "member", [(i, chips - 1 - i) for i in range(chips)])
    rim_near, rim_far, grad_grid0, _ = lax.optimization_barrier(
        (rim_near, rim_far, grad_grid0, send)
    )
    got_far = lax.ppermute(rim_far, "space", second)
    got_near = lax.ppermute(rim_near, "space", first)
    owned, edge0 = owned_of(0, grad_grid0, None)
    got, _ = lax.optimization_barrier((got, edge0))
    kept, send = halve(kept, got, 1)
    got = lax.ppermute(send, "member", [(i, i ^ 1) for i in range(chips)])
    grad_grid1, _ = lax.optimization_barrier((grad_grid1, send))
    owned, edge1 = owned_of(1, grad_grid1, owned)
    got, _ = lax.optimization_barrier((got, edge1))

    last_rows = quarter // spaces
    spread = pl.pallas_call(
        scatter_kernel,
        in_specs=[vmem()] * 2,
        out_specs=vmem(),
        out_shape=shape((spaces, last_rows, wide), bf16),
        compiler_params=params(8),
    )(kept, got)
    spread = lax.all_to_all(spread, "space", 0, 0, tiled=True)
    grad_latent, grad_w_in, grad_w_out = pl.pallas_call(
        finish_kernel,
        in_specs=[hbm()] + [vmem()] * 5,
        out_specs=[hbm(), vmem(), vmem()],
        out_shape=[
            shape(owned.shape, f32),
            shape((last_rows, feature), f32),
            shape((last_rows, variables), f32),
        ],
        scratch_shapes=[
            pltpu.VMEM((2 * members, edge_rows, feature), f32),
            pltpu.SemaphoreType.DMA((2 * members,)),
        ],
        input_output_aliases={0: 0},
        compiler_params=params(8),
    )(owned, *in_vmem(edge0, edge1), got_near, got_far, spread)
    return grad_latent[None], grad_w_in, grad_w_out.T


def solution(mesh):
    placed = (
        P("dp", "member", "space", None),
        P("space", None, None, None),
        P("space", None),
        P("space"),
        P(),
        P(),
        P("dp", None, "space"),
        P("space"),
        P(),
    )
    return jax.shard_map(
        local,
        mesh=mesh,
        in_specs=placed,
        out_specs=(
            P("dp", "member", "space", None),
            P(("dp", "member", "space"), None),
            P(None, ("dp", "member", "space")),
        ),
        check_vma=False,
    )
```

```python
import functools

import jax
import jax.numpy as jnp
from jax import lax
from jax.experimental import pallas as pl
from jax.experimental.pallas import tpu as pltpu
from jax.sharding import PartitionSpec as P

HALO = 2
smooth_square = 0.1 * 0.1
gelu_scale = 0.7978845608028654
gelu_cubic = 0.044715
MIB = 1 << 20
f32 = jnp.float32
bf16 = jnp.bfloat16

NN = (((1,), (0,)), ((), ()))
NT = (((1,), (1,)), ((), ()))


def dot(a, b, dims=NN):
    return lax.dot_general(a, b, dims, preferred_element_type=f32)


def vmem():
    return pl.BlockSpec(memory_space=pltpu.VMEM)


def smem():
    return pl.BlockSpec(memory_space=pltpu.SMEM)


def hbm():
    return pl.BlockSpec(memory_space=pltpu.HBM)


def in_hbm(x):
    return pltpu.with_memory_space_constraint(x, pltpu.HBM)


def in_vmem(*xs):
    return [pltpu.with_memory_space_constraint(x, pltpu.VMEM) for x in xs]


def held(dims, dtype):
    return pltpu.VMEM(dims, dtype)


def anywhere():
    return pl.BlockSpec(memory_space=pl.ANY)


def cost(mega):
    return pl.CostEstimate(flops=mega * 1_000_000, bytes_accessed=mega * 4000, transcendentals=0)


def params(mib):
    return pltpu.CompilerParams(vmem_limit_bytes=mib * MIB)


def shape(dims, dtype):
    return jax.ShapeDtypeStruct(dims, dtype)


def rows_at(start, size):
    return pl.ds(pl.multiple_of(start * size, size), size)


def parity():
    return lax.rem(lax.axis_index("space") + 1, 2)


def edges_kernel(lat, near0, far0, near1, far1, sems):
    step = near0.shape[0]
    last = lat.shape[1] - step
    odd = parity()
    top = pl.multiple_of((1 - odd) * last, step)
    bottom = pl.multiple_of(odd * last, step)
    copies = []
    for m, (near, far) in enumerate(((near0, far0), (near1, far1))):
        for out, start in ((near, top), (far, bottom)):
            copies.append(
                pltpu.make_async_copy(lat.at[m, pl.ds(start, step)], out, sems.at[len(copies)])
            )
            copies[-1].start()
    for copy in copies:
        copy.wait()


def halo_slot(e, blocks, spaces):
    at_space = lax.axis_index("space")
    odd = parity()
    below, above = e < HALO, e >= HALO + blocks
    outside = (below & (at_space > 0)) | (above & (at_space < spaces - 1))
    slot = jnp.where(below, e + (1 - odd) * HALO, e - HALO - blocks + odd * HALO)
    return outside, jnp.where(below | above, slot, 0)


def prepare_kernel(
    ids_hbm, count_hbm, lat_hbm, weight_hbm, w_in_hbm, w_out,
    acc0, acc1, halo_w, w_in_v, w_out_v, weight, ids, count, lat, sems, *, spaces,
):
    tiles, slots, cells, nodes = weight.shape
    blocks = lat.shape[1]
    copies = [
        pltpu.make_async_copy(ids_hbm, ids, sems.at[4]),
        pltpu.make_async_copy(count_hbm, count, sems.at[5]),
        pltpu.make_async_copy(weight_hbm, weight, sems.at[0]),
        pltpu.make_async_copy(lat_hbm.at[0], lat.at[0], sems.at[1]),
        pltpu.make_async_copy(lat_hbm.at[1], lat.at[1], sems.at[2]),
        pltpu.make_async_copy(w_in_hbm, w_in_v, sems.at[3]),
    ]
    for c in copies:
        c.start()
    halo_w[...] = jnp.zeros_like(halo_w)
    w_out_v[...] = jnp.zeros_like(w_out_v)
    w_out_v[: w_out.shape[0]] = w_out[...]
    for c in copies[:3]:
        c.wait()

    unused = halo_w.shape[1] // nodes - 1
    for t in range(tiles):
        rows = slice(t * cells, (t + 1) * cells)
        for k in range(slots):
            outside, slot = halo_slot(ids[k, t], blocks, spaces)
            slot = jnp.where((k < count[t]) & outside, slot, unused)
            halo_w[rows, rows_at(slot, nodes)] += weight[t, k]

    for m, acc in enumerate((acc0, acc1)):
        copies[3 + m].wait()
        for t in range(tiles):
            parts, at = [], []
            for k in range(slots):
                e = ids[k, t]
                mine = (k < count[t]) & (e >= HALO) & (e < HALO + blocks)
                w = weight[t, k]
                parts.append(jnp.where(mine, w, jnp.zeros_like(w)))
                at.append(jnp.clip(e - HALO, 0, blocks - 1))
            lhs = jnp.concatenate(parts, axis=1)
            rhs = jnp.concatenate([lat[m, a] for a in at], axis=0)
            acc[t * cells : (t + 1) * cells] = dot(lhs, rhs)
    copies[5].wait()


def turn_kernel(
    ids, count, weight, w_in, w_out, target, var_weight, later,
    turned, w_in_t, w_out_t, target_v, scale_v, square, *, spaces, blocks,
):
    tiles, slots, cells, nodes = weight.shape
    turned[...] = jnp.zeros_like(turned)
    w_in_t[...] = w_in[...].T
    w_out_t[...] = w_out[...].T
    variables = target.shape[0]
    target_v[...] = jnp.zeros_like(target_v)
    target_v[:variables] = target[...]
    square[...] = jnp.zeros_like(square)
    square[:1, :variables] = var_weight[...]
    scale_v[...] = square[...].T[: scale_v.shape[0], :1]
    unused = turned.shape[0] // nodes - 1
    for t in range(tiles):
        columns = slice(t * cells, (t + 1) * cells)
        for k in range(slots):
            e = ids[k, t]
            outside, slot = halo_slot(e, blocks, spaces)
            mine = (e >= HALO) & (e < HALO + blocks)
            block = jnp.where(mine, e - HALO, jnp.where(outside, blocks + slot, unused))
            block = jnp.where(k < count[t], block, unused)
            turned[rows_at(block, nodes), columns] += weight[t, k].T


def gelu_parts(x):
    square = x * x
    half = 0.5 + 0.5 * jnp.tanh(x * (gelu_scale + (gelu_scale * gelu_cubic) * square))
    return square, half


CHUNK = 256


def fields_kernel(acc, near, far, halo_w, w_in, w_out, lat_out, fields):
    count = acc.shape[0]
    half_k = near.shape[0]
    for start in range(0, count, 2 * CHUNK):
        at = slice(start, start + 2 * CHUNK)
        total = acc[at] + dot(halo_w[at, :half_k], near[...])
        total = total + dot(halo_w[at, half_k : 2 * half_k], far[...])
        rounded = total.astype(bf16)
        lat_out[at] = rounded
        pre = dot(w_in[...], rounded, NT)
        _, half = gelu_parts(pre)
        fields[:, at] = dot(w_out[...], (pre * half).astype(bf16)).astype(bf16)


def slopes_kernel(lat, w_in, act_t, slope_t):
    count = lat.shape[0]
    for start in range(0, count, CHUNK):
        at = slice(start, start + CHUNK)
        x = dot(w_in[...], lat[at], NT)
        square, half = gelu_parts(x)
        act_t[:, at] = (x * half).astype(bf16)
        inner = x * (2.0 * gelu_scale + (6.0 * gelu_scale * gelu_cubic) * square)
        slope_t[:, at] = (half + half * (1.0 - half) * inner).astype(bf16)


def smooth_sign(u):
    return u * lax.rsqrt(u * u + smooth_square)


def spread_kernel(
    own0, own1, o10, o11, o20, o21, far0, target, part0, part1, *, ensemble,
):
    count = own0.shape[1]
    for start in range(0, count, CHUNK):
        at = slice(start, start + CHUNK)
        truth = target[:, at].astype(f32)
        mine = [own0[:, at].astype(f32), own1[:, at].astype(f32)]
        pair = smooth_sign(mine[0] - mine[1])
        spread = [pair, -pair]
        for other in (o10, o11, o20, o21, far0):
            theirs = other[:, at].astype(f32)
            for a in range(2):
                spread[a] = spread[a] + smooth_sign(mine[a] - theirs)
        for a, part in enumerate((part0, part1)):
            value = smooth_sign(mine[a] - truth) * (1.0 / ensemble)
            part[:, at] = value - spread[a] * (1.0 / (ensemble * (ensemble - 1)))


def weights_kernel(
    own0, own1, far1, part0, part1, area, var_weight,
    act0, act1, slope0, slope1, lat0, lat1, w_out_t,
    grad_pre0, grad_pre1, keep, send, total_in, total_out, *, ensemble, states,
):
    count = own0.shape[1]
    for start in range(0, count, CHUNK):
        at = slice(start, start + CHUNK)
        mine = [own0[:, at].astype(f32), own1[:, at].astype(f32)]
        theirs = far1[:, at].astype(f32)
        cell_weight = area[:, at] * var_weight[...] * (1.0 / states)
        cots = []
        for a, part in enumerate((part0, part1)):
            spread = smooth_sign(mine[a] - theirs)
            value = part[:, at] - spread * (1.0 / (ensemble * (ensemble - 1)))
            cots.append((cell_weight * value).astype(bf16))
        cot = jnp.concatenate(cots, axis=1)
        grad_act = dot(w_out_t[...], cot)
        slope = jnp.concatenate([slope0[:, at], slope1[:, at]], axis=1)
        pre = (grad_act * slope.astype(f32)).astype(bf16)
        grad_pre0[:, at] = pre[:, :CHUNK]
        grad_pre1[:, at] = pre[:, CHUNK:]
        part_in = dot(pre, jnp.concatenate([lat0[at], lat1[at]], axis=0))
        act = jnp.concatenate([act0[:, at], act1[:, at]], axis=1)
        part_out = dot(act, cot, NT)
        if start == 0:
            total_in[...] = part_in
            total_out[...] = jnp.zeros_like(total_out)
            total_out[:, : part_out.shape[1]] = part_out
        else:
            total_in[...] += part_in
            total_out[:, : part_out.shape[1]] += part_out
    rows = keep.shape[0]
    wide = total_in.shape[1]
    here = lax.axis_index("dp")
    stay, leave = rows_at(here, rows), rows_at(1 - here, rows)
    keep[:, :wide] = total_in[stay]
    keep[:, wide:] = total_out[stay]
    send[:, :wide] = total_in[leave].astype(bf16)
    send[:, wide:] = total_out[leave].astype(bf16)


def rim_kernel(
    grad_pre0, grad_pre1, turned, w_in_t, grad_grid0, grad_grid1, near, far, *, own_rows,
):
    half_k = near.shape[1]
    middle = own_rows + half_k
    for m, (grad_pre, grad_grid) in enumerate(
        ((grad_pre0, grad_grid0), (grad_pre1, grad_grid1))
    ):
        grad_grid[...] = dot(w_in_t[...], grad_pre[...]).astype(bf16)
        near[m] = dot(turned[own_rows:middle], grad_grid[...], NT).astype(bf16)
        far[m] = dot(turned[middle : middle + half_k], grad_grid[...], NT).astype(bf16)


def owned_kernel(grad_grid, turned, base, out, edge, parts, sems, *, member, own_rows):
    step, size = edge.shape[1], parts.shape[1]
    copies = []
    for slot in range(parts.shape[0]):
        start = step + slot * size
        parts[slot] = dot(turned[start : start + size], grad_grid[...], NT)
        copy = pltpu.make_async_copy(
            parts.at[slot], out.at[member, start : start + size], sems.at[slot]
        )
        copy.start()
        copies.append(copy)
    ends = jnp.concatenate([turned[:step], turned[own_rows - step : own_rows]], axis=0)
    value = dot(ends, grad_grid[...], NT)
    edge[0] = value[:step]
    edge[1] = value[step:]
    for copy in copies:
        copy.wait()


def finish_kernel(
    base, edge0, edge1, near, far, got, out, grad_in, grad_out, parts, sems,
):
    step = edge0.shape[1]
    last = out.shape[1] - step
    odd = parity()
    copies = []
    for side, rim in ((1 - odd, near), (odd, far)):
        start = pl.multiple_of(side * last, step)
        for m, edge in enumerate((edge0, edge1)):
            slot = len(copies)
            parts[slot] = edge[side] + rim[m].astype(f32)
            copy = pltpu.make_async_copy(
                parts.at[slot], out.at[m, pl.ds(start, step)], sems.at[slot]
            )
            copy.start()
            copies.append(copy)
    value = got[0].astype(f32)
    for p in range(1, got.shape[0]):
        value = value + got[p].astype(f32)
    wide = grad_in.shape[1]
    grad_in[...] = value[:, :wide]
    grad_out[...] = value[:, wide : wide + grad_out.shape[1]]
    for copy in copies:
        copy.wait()


def halve_kernel(kept, got, keep, send, total, *, bit):
    rows = keep.shape[0]
    total[...] = kept[...] + got[...].astype(f32)
    here = lax.rem(lax.axis_index("member") // bit, 2)
    keep[...] = total[rows_at(here, rows)]
    send[...] = total[rows_at(1 - here, rows)].astype(send.dtype)


def halve(kept, got, bit):
    rows, wide = kept.shape[0] // 2, kept.shape[1]
    return pl.pallas_call(
        functools.partial(halve_kernel, bit=bit),
        in_specs=[vmem()] * 2,
        out_specs=[vmem()] * 2,
        out_shape=[shape((rows, wide), f32), shape((rows, wide), bf16)],
        scratch_shapes=[pltpu.VMEM(kept.shape, f32)],
        compiler_params=params(8),
        cost_estimate=cost(2000),
    )(kept, got)


def scatter_kernel(kept, got, out):
    value = kept[...] + got[...].astype(f32)
    parts, rows = out.shape[0], out.shape[1]
    for p in range(parts):
        out[p] = value[p * rows : (p + 1) * rows].astype(out.dtype)


def ring(count, distance):
    return [(i, (i + distance) % count) for i in range(count)]


def local(latents, edge_weight, block_ids, block_count, w_in, w_out, targets, area, var_weight):
    members = latents.shape[1]
    feature = latents.shape[3]
    hidden = w_in.shape[0]
    variables = w_out.shape[0]
    rows_v = (variables + 7) // 8 * 8
    tiles, slots, cells, nodes = edge_weight.shape
    n = tiles * cells
    lat = latents[0].reshape(members, -1, nodes, feature)
    blocks = lat.shape[1]
    edge_rows = HALO * nodes
    rim_rows = 2 * edge_rows
    spaces = lax.axis_size("space")
    chips = lax.axis_size("member")
    ids = block_ids.T
    first = [(i, (((i + 1) ^ 1) - 1) % spaces) for i in range(spaces)]
    second = [(i, i ^ 1) for i in range(spaces)]

    edges = pl.pallas_call(
        edges_kernel,
        in_specs=[hbm()],
        out_specs=[vmem()] * 4,
        out_shape=[shape((edge_rows, feature), bf16)] * 4,
        scratch_shapes=[pltpu.SemaphoreType.DMA((4,))],
        compiler_params=params(8),
    )(in_hbm(latents[0]))
    halos = []
    for m in range(members):
        far = lax.ppermute(edges[2 * m + 1], "space", second)
        near = lax.ppermute(edges[2 * m], "space", first)
        halos.append((near, far))

    scale_n = area[None, :]

    acc0, acc1, halo_w, w_in_v, w_out_v, weight_v = pl.pallas_call(
        functools.partial(prepare_kernel, spaces=spaces),
        in_specs=[hbm()] * 5 + [vmem()],
        out_specs=[vmem()] * 6,
        out_shape=[
            held((n, feature), f32),
            held((n, feature), f32),
            held((n, rim_rows + nodes), bf16),
            held((hidden, feature), bf16),
            held((rows_v, hidden), bf16),
            held(edge_weight.shape, bf16),
        ],
        scratch_shapes=[
            pltpu.SMEM(ids.shape, jnp.int32),
            pltpu.SMEM(block_count.shape, jnp.int32),
            pltpu.VMEM(lat.shape, bf16),
            pltpu.SemaphoreType.DMA((6,)),
        ],
        compiler_params=params(12),
        cost_estimate=cost(2000),
    )(
        in_hbm(ids), in_hbm(block_count), in_hbm(lat), in_hbm(edge_weight), in_hbm(w_in),
        in_hbm(w_out),
    )

    def along(x, distance):
        return lax.ppermute(x, "member", ring(chips, distance))

    def fields_of(acc, near, far):
        return pl.pallas_call(
            fields_kernel,
            in_specs=[vmem()] * 6,
            out_specs=[vmem()] * 2,
            out_shape=[held((n, feature), bf16), shape((rows_v, n), bf16)],
            compiler_params=params(8),
            cost_estimate=cost(100),
        )(*in_vmem(acc), near, far, *in_vmem(halo_w, w_in_v, w_out_v))

    def slopes_of(lat_m):
        return pl.pallas_call(
            slopes_kernel,
            in_specs=[vmem()] * 2,
            out_specs=[vmem()] * 2,
            out_shape=[held((hidden, n), bf16)] * 2,
            compiler_params=params(8),
            cost_estimate=cost(100),
        )(*in_vmem(lat_m, w_in_v))

    lat0, fields0 = fields_of(acc0, *halos[0])
    left0 = along(fields0, 1)
    right0 = along(fields0, -1)
    lat1, fields1 = fields_of(acc1, *halos[1])
    right1 = along(fields1, -1)
    left1 = along(fields1, 1)
    fields = [fields0, fields1]
    first_lat, left0, right0 = lax.optimization_barrier((lat0, left0, right0))
    act0, slope0 = slopes_of(first_lat)
    far0 = along(left0, 1)
    second_lat, _ = lax.optimization_barrier((lat1, slope0))
    act1, slope1 = slopes_of(second_lat)
    held_right1, _ = lax.optimization_barrier((right1, slope0))
    far1 = along(held_right1, -1)
    grid_latent, acts, slopes = [lat0, lat1], [act0, act1], [slope0, slope1]

    own_rows = blocks * nodes
    turned, w_in_t, w_out_t, target, scale_v = pl.pallas_call(
        functools.partial(turn_kernel, spaces=spaces, blocks=blocks),
        in_specs=[smem(), smem()] + [vmem()] * 5 + [anywhere()],
        out_specs=[vmem()] * 5,
        out_shape=[
            held((own_rows + rim_rows + nodes, n), bf16),
            held((feature, hidden), bf16),
            held((hidden, rows_v), bf16),
            held((rows_v, n), bf16),
            held((rows_v, 1), f32),
        ],
        scratch_shapes=[pltpu.VMEM((128, 128), f32)],
        compiler_params=params(8),
        cost_estimate=cost(100),
    )(
        ids, block_count, *in_vmem(weight_v, w_in_v, w_out_v), targets[0], var_weight[None],
        slopes[1],
    )

    part0, part1 = pl.pallas_call(
        functools.partial(spread_kernel, ensemble=members * chips),
        in_specs=[vmem()] * 8,
        out_specs=[vmem()] * 2,
        out_shape=[held((rows_v, n), f32)] * 2,
        compiler_params=params(8),
        cost_estimate=cost(100),
    )(*fields, left0, left1, right0, right1, far0, *in_vmem(target))

    wide = feature + 128
    half_rows = hidden // 2
    grad_pre0, grad_pre1, keep, send = pl.pallas_call(
        functools.partial(
            weights_kernel,
            ensemble=members * chips,
            states=targets.shape[0] * lax.axis_size("dp"),
        ),
        in_specs=[vmem()] * 14,
        out_specs=[vmem()] * 4,
        out_shape=[
            held((hidden, n), bf16),
            held((hidden, n), bf16),
            shape((half_rows, wide), f32),
            shape((half_rows, wide), bf16),
        ],
        scratch_shapes=[pltpu.VMEM((hidden, feature), f32), pltpu.VMEM((hidden, 128), f32)],
        compiler_params=params(12),
        cost_estimate=cost(2000),
    )(
        *fields, far1, *in_vmem(part0, part1), scale_n, *in_vmem(scale_v),
        *in_vmem(*acts, *slopes, *grid_latent, w_out_t),
    )

    swapped = lax.ppermute(send, "dp", [(0, 1), (1, 0)])

    grad_grid0, grad_grid1, rim_near, rim_far = pl.pallas_call(
        functools.partial(rim_kernel, own_rows=own_rows),
        in_specs=[vmem()] * 4,
        out_specs=[vmem()] * 4,
        out_shape=[held((feature, n), bf16)] * 2 + [shape((members, edge_rows, feature), bf16)] * 2,
        compiler_params=params(8),
        cost_estimate=cost(2000),
    )(*in_vmem(grad_pre0, grad_pre1, turned, w_in_t))

    quarter = half_rows // chips
    pieces = 3
    size = (own_rows - 2 * edge_rows) // pieces

    def owned_of(member, grad_grid, base):
        whole = shape((members, blocks * nodes, feature), f32)
        aliased = {} if base is None else {2: 0}
        base = grad_grid if base is None else base
        return pl.pallas_call(
            functools.partial(owned_kernel, member=member, own_rows=own_rows),
            in_specs=[vmem()] * 2 + [anywhere()],
            out_specs=[hbm(), vmem()],
            out_shape=[whole, held((2, edge_rows, feature), f32)],
            scratch_shapes=[
                pltpu.VMEM((pieces, size, feature), f32),
                pltpu.SemaphoreType.DMA((pieces,)),
            ],
            input_output_aliases=aliased,
            compiler_params=params(8),
            cost_estimate=cost(2000),
        )(*in_vmem(grad_grid, turned), base)

    swapped, _ = lax.optimization_barrier((swapped, grad_grid0))
    kept, send = halve(keep, swapped, 2)
    got = lax.ppermute(send, "member", [(i, chips - 1 - i) for i in range(chips)])
    rim_near, rim_far, grad_grid0, _ = lax.optimization_barrier(
        (rim_near, rim_far, grad_grid0, send)
    )
    got_far = lax.ppermute(rim_far, "space", second)
    got_near = lax.ppermute(rim_near, "space", first)
    owned, edge0 = owned_of(0, grad_grid0, None)
    got, _ = lax.optimization_barrier((got, edge0))
    kept, send = halve(kept, got, 1)
    got = lax.ppermute(send, "member", [(i, i ^ 1) for i in range(chips)])
    grad_grid1, _ = lax.optimization_barrier((grad_grid1, send))
    owned, edge1 = owned_of(1, grad_grid1, owned)
    got, _ = lax.optimization_barrier((got, edge1))

    last_rows = quarter // spaces
    spread = pl.pallas_call(
        scatter_kernel,
        in_specs=[vmem()] * 2,
        out_specs=vmem(),
        out_shape=shape((spaces, last_rows, wide), bf16),
        compiler_params=params(8),
    )(kept, got)
    spread = lax.all_to_all(spread, "space", 0, 0, tiled=True)
    grad_latent, grad_w_in, grad_w_out = pl.pallas_call(
        finish_kernel,
        in_specs=[hbm()] + [vmem()] * 5,
        out_specs=[hbm(), vmem(), vmem()],
        out_shape=[
            shape(owned.shape, f32),
            shape((last_rows, feature), f32),
            shape((last_rows, variables), f32),
        ],
        scratch_shapes=[
            pltpu.VMEM((2 * members, edge_rows, feature), f32),
            pltpu.SemaphoreType.DMA((2 * members,)),
        ],
        input_output_aliases={0: 0},
        compiler_params=params(8),
    )(owned, *in_vmem(edge0, edge1), got_near, got_far, spread)
    return grad_latent[None], grad_w_in, grad_w_out.T


def solution(mesh):
    placed = (
        P("dp", "member", "space", None),
        P("space", None, None, None),
        P("space", None),
        P("space"),
        P(),
        P(),
        P("dp", None, "space"),
        P("space"),
        P(),
    )
    return jax.shard_map(
        local,
        mesh=mesh,
        in_specs=placed,
        out_specs=(
            P("dp", "member", "space", None),
            P(("dp", "member", "space"), None),
            P(None, ("dp", "member", "space")),
        ),
        check_vma=False,
    )
```

```python
import functools

import jax
import jax.numpy as jnp
from jax import lax
from jax.experimental import pallas as pl
from jax.experimental.pallas import tpu as pltpu
from jax.sharding import PartitionSpec as P

HALO = 2
smooth_square = 0.1 * 0.1
gelu_scale = 0.7978845608028654
gelu_cubic = 0.044715
MIB = 1 << 20
f32 = jnp.float32
bf16 = jnp.bfloat16

NN = (((1,), (0,)), ((), ()))
NT = (((1,), (1,)), ((), ()))


def dot(a, b, dims=NN):
    return lax.dot_general(a, b, dims, preferred_element_type=f32)


def vmem():
    return pl.BlockSpec(memory_space=pltpu.VMEM)


def smem():
    return pl.BlockSpec(memory_space=pltpu.SMEM)


def hbm():
    return pl.BlockSpec(memory_space=pltpu.HBM)


def in_hbm(x):
    return pltpu.with_memory_space_constraint(x, pltpu.HBM)


def in_vmem(*xs):
    return [pltpu.with_memory_space_constraint(x, pltpu.VMEM) for x in xs]


def held(dims, dtype):
    return pltpu.VMEM(dims, dtype)


def anywhere():
    return pl.BlockSpec(memory_space=pl.ANY)


def cost(mega):
    return pl.CostEstimate(flops=mega * 1_000_000, bytes_accessed=mega * 4000, transcendentals=0)


def params(mib):
    return pltpu.CompilerParams(vmem_limit_bytes=mib * MIB)


def shape(dims, dtype):
    return jax.ShapeDtypeStruct(dims, dtype)


def rows_at(start, size):
    return pl.ds(pl.multiple_of(start * size, size), size)


def parity():
    return lax.rem(lax.axis_index("space") + 1, 2)


def edges_kernel(lat, near0, far0, near1, far1, sems):
    step = near0.shape[0]
    last = lat.shape[1] - step
    odd = parity()
    top = pl.multiple_of((1 - odd) * last, step)
    bottom = pl.multiple_of(odd * last, step)
    copies = []
    for m, (near, far) in enumerate(((near0, far0), (near1, far1))):
        for out, start in ((near, top), (far, bottom)):
            copies.append(
                pltpu.make_async_copy(lat.at[m, pl.ds(start, step)], out, sems.at[len(copies)])
            )
            copies[-1].start()
    for copy in copies:
        copy.wait()


def halo_slot(e, blocks, spaces):
    at_space = lax.axis_index("space")
    odd = parity()
    below, above = e < HALO, e >= HALO + blocks
    outside = (below & (at_space > 0)) | (above & (at_space < spaces - 1))
    slot = jnp.where(below, e + (1 - odd) * HALO, e - HALO - blocks + odd * HALO)
    return outside, jnp.where(below | above, slot, 0)


def prepare_kernel(
    ids_hbm, count_hbm, lat_hbm, weight_hbm, w_in_hbm, w_out,
    acc0, acc1, halo_w, w_in_v, w_out_v, weight, ids, count, lat, sems, *, spaces,
):
    tiles, slots, cells, nodes = weight.shape
    blocks = lat.shape[1]
    copies = [
        pltpu.make_async_copy(ids_hbm, ids, sems.at[4]),
        pltpu.make_async_copy(count_hbm, count, sems.at[5]),
        pltpu.make_async_copy(weight_hbm, weight, sems.at[0]),
        pltpu.make_async_copy(lat_hbm.at[0], lat.at[0], sems.at[1]),
        pltpu.make_async_copy(lat_hbm.at[1], lat.at[1], sems.at[2]),
        pltpu.make_async_copy(w_in_hbm, w_in_v, sems.at[3]),
    ]
    for c in copies:
        c.start()
    halo_w[...] = jnp.zeros_like(halo_w)
    w_out_v[...] = jnp.zeros_like(w_out_v)
    w_out_v[: w_out.shape[0]] = w_out[...]
    for c in copies[:3]:
        c.wait()

    unused = halo_w.shape[1] // nodes - 1
    for t in range(tiles):
        rows = slice(t * cells, (t + 1) * cells)
        for k in range(slots):
            outside, slot = halo_slot(ids[k, t], blocks, spaces)
            slot = jnp.where((k < count[t]) & outside, slot, unused)
            halo_w[rows, rows_at(slot, nodes)] += weight[t, k]

    for m, acc in enumerate((acc0, acc1)):
        copies[3 + m].wait()
        for t in range(tiles):
            parts, at = [], []
            for k in range(slots):
                e = ids[k, t]
                mine = (k < count[t]) & (e >= HALO) & (e < HALO + blocks)
                w = weight[t, k]
                parts.append(jnp.where(mine, w, jnp.zeros_like(w)))
                at.append(jnp.clip(e - HALO, 0, blocks - 1))
            lhs = jnp.concatenate(parts, axis=1)
            rhs = jnp.concatenate([lat[m, a] for a in at], axis=0)
            acc[t * cells : (t + 1) * cells] = dot(lhs, rhs)
    copies[5].wait()


def turn_kernel(
    ids, count, weight, w_in, w_out, target, var_weight, later,
    turned, w_in_t, w_out_t, target_v, scale_v, square, *, spaces, blocks,
):
    tiles, slots, cells, nodes = weight.shape
    turned[...] = jnp.zeros_like(turned)
    w_in_t[...] = w_in[...].T
    w_out_t[...] = w_out[...].T
    variables = target.shape[0]
    target_v[...] = jnp.zeros_like(target_v)
    target_v[:variables] = target[...]
    square[...] = jnp.zeros_like(square)
    square[:1, :variables] = var_weight[...]
    scale_v[...] = square[...].T[: scale_v.shape[0], :1]
    unused = turned.shape[0] // nodes - 1
    for t in range(tiles):
        columns = slice(t * cells, (t + 1) * cells)
        for k in range(slots):
            e = ids[k, t]
            outside, slot = halo_slot(e, blocks, spaces)
            mine = (e >= HALO) & (e < HALO + blocks)
            block = jnp.where(mine, e - HALO, jnp.where(outside, blocks + slot, unused))
            block = jnp.where(k < count[t], block, unused)
            turned[rows_at(block, nodes), columns] += weight[t, k].T


def gelu_parts(x):
    square = x * x
    half = 0.5 + 0.5 * jnp.tanh(x * (gelu_scale + (gelu_scale * gelu_cubic) * square))
    return square, half


CHUNK = 256


def fields_kernel(acc, near, far, halo_w, w_in, w_out, lat_out, fields):
    count = acc.shape[0]
    half_k = near.shape[0]
    for start in range(0, count, 4 * CHUNK):
        at = slice(start, start + 4 * CHUNK)
        total = acc[at] + dot(halo_w[at, :half_k], near[...])
        total = total + dot(halo_w[at, half_k : 2 * half_k], far[...])
        rounded = total.astype(bf16)
        lat_out[at] = rounded
        pre = dot(w_in[...], rounded, NT)
        _, half = gelu_parts(pre)
        fields[:, at] = dot(w_out[...], (pre * half).astype(bf16)).astype(bf16)


def slopes_kernel(lat, w_in, act_t, slope_t):
    count = lat.shape[0]
    for start in range(0, count, CHUNK):
        at = slice(start, start + CHUNK)
        x = dot(w_in[...], lat[at], NT)
        square, half = gelu_parts(x)
        act_t[:, at] = (x * half).astype(bf16)
        inner = x * (2.0 * gelu_scale + (6.0 * gelu_scale * gelu_cubic) * square)
        slope_t[:, at] = (half + half * (1.0 - half) * inner).astype(bf16)


def smooth_sign(u):
    return u * lax.rsqrt(u * u + smooth_square)


def spread_kernel(
    own0, own1, o10, o11, o20, o21, far0, target, part0, part1, *, ensemble,
):
    count = own0.shape[1]
    for start in range(0, count, CHUNK):
        at = slice(start, start + CHUNK)
        truth = target[:, at].astype(f32)
        mine = [own0[:, at].astype(f32), own1[:, at].astype(f32)]
        pair = smooth_sign(mine[0] - mine[1])
        spread = [pair, -pair]
        for other in (o10, o11, o20, o21, far0):
            theirs = other[:, at].astype(f32)
            for a in range(2):
                spread[a] = spread[a] + smooth_sign(mine[a] - theirs)
        for a, part in enumerate((part0, part1)):
            value = smooth_sign(mine[a] - truth) * (1.0 / ensemble)
            part[:, at] = value - spread[a] * (1.0 / (ensemble * (ensemble - 1)))


def weights_kernel(
    own0, own1, far1, part0, part1, area, var_weight,
    act0, act1, slope0, slope1, lat0, lat1, w_out_t,
    grad_pre0, grad_pre1, keep, send, total_in, total_out, *, ensemble, states,
):
    count = own0.shape[1]
    for start in range(0, count, CHUNK):
        at = slice(start, start + CHUNK)
        mine = [own0[:, at].astype(f32), own1[:, at].astype(f32)]
        theirs = far1[:, at].astype(f32)
        cell_weight = area[:, at] * var_weight[...] * (1.0 / states)
        cots = []
        for a, part in enumerate((part0, part1)):
            spread = smooth_sign(mine[a] - theirs)
            value = part[:, at] - spread * (1.0 / (ensemble * (ensemble - 1)))
            cots.append((cell_weight * value).astype(bf16))
        cot = jnp.concatenate(cots, axis=1)
        grad_act = dot(w_out_t[...], cot)
        slope = jnp.concatenate([slope0[:, at], slope1[:, at]], axis=1)
        pre = (grad_act * slope.astype(f32)).astype(bf16)
        grad_pre0[:, at] = pre[:, :CHUNK]
        grad_pre1[:, at] = pre[:, CHUNK:]
        part_in = dot(pre, jnp.concatenate([lat0[at], lat1[at]], axis=0))
        act = jnp.concatenate([act0[:, at], act1[:, at]], axis=1)
        part_out = dot(act, cot, NT)
        if start == 0:
            total_in[...] = part_in
            total_out[...] = jnp.zeros_like(total_out)
            total_out[:, : part_out.shape[1]] = part_out
        else:
            total_in[...] += part_in
            total_out[:, : part_out.shape[1]] += part_out
    rows = keep.shape[0]
    wide = total_in.shape[1]
    here = lax.axis_index("dp")
    stay, leave = rows_at(here, rows), rows_at(1 - here, rows)
    keep[:, :wide] = total_in[stay]
    keep[:, wide:] = total_out[stay]
    send[:, :wide] = total_in[leave].astype(bf16)
    send[:, wide:] = total_out[leave].astype(bf16)


def rim_kernel(
    grad_pre0, grad_pre1, turned, w_in_t, grad_grid0, grad_grid1, near, far, *, own_rows,
):
    half_k = near.shape[1]
    for m, (grad_pre, grad_grid) in enumerate(
        ((grad_pre0, grad_grid0), (grad_pre1, grad_grid1))
    ):
        grad_grid[...] = dot(w_in_t[...], grad_pre[...]).astype(bf16)
        rims = dot(turned[own_rows : own_rows + 2 * half_k], grad_grid[...], NT).astype(bf16)
        near[m] = rims[:half_k]
        far[m] = rims[half_k:]


def owned_kernel(grad_grid, turned, base, out, edge, parts, sems, *, member, own_rows):
    step, size = edge.shape[1], parts.shape[1]
    copies = []
    for slot in range(parts.shape[0]):
        start = step + slot * size
        parts[slot] = dot(turned[start : start + size], grad_grid[...], NT)
        copy = pltpu.make_async_copy(
            parts.at[slot], out.at[member, start : start + size], sems.at[slot]
        )
        copy.start()
        copies.append(copy)
    ends = jnp.concatenate([turned[:step], turned[own_rows - step : own_rows]], axis=0)
    value = dot(ends, grad_grid[...], NT)
    edge[0] = value[:step]
    edge[1] = value[step:]
    for copy in copies:
        copy.wait()


def finish_kernel(
    base, edge0, edge1, far, near, got, out, grad_in, grad_out, parts, sems,
):
    step = edge0.shape[1]
    last = out.shape[1] - step
    odd = parity()
    copies = []
    for side, rim in ((1 - odd, near), (odd, far)):
        start = pl.multiple_of(side * last, step)
        for m, edge in enumerate((edge0, edge1)):
            slot = len(copies)
            parts[slot] = edge[side] + rim[m].astype(f32)
            copy = pltpu.make_async_copy(
                parts.at[slot], out.at[m, pl.ds(start, step)], sems.at[slot]
            )
            copy.start()
            copies.append(copy)
    value = got[0].astype(f32)
    for p in range(1, got.shape[0]):
        value = value + got[p].astype(f32)
    wide = grad_in.shape[1]
    grad_in[...] = value[:, :wide]
    grad_out[...] = value[:, wide : wide + grad_out.shape[1]]
    for copy in copies:
        copy.wait()


def halve_kernel(kept, got, keep, send, total, *, bit):
    rows = keep.shape[0]
    total[...] = kept[...] + got[...].astype(f32)
    here = lax.rem(lax.axis_index("member") // bit, 2)
    keep[...] = total[rows_at(here, rows)]
    send[...] = total[rows_at(1 - here, rows)].astype(send.dtype)


def halve(kept, got, bit):
    rows, wide = kept.shape[0] // 2, kept.shape[1]
    return pl.pallas_call(
        functools.partial(halve_kernel, bit=bit),
        in_specs=[vmem()] * 2,
        out_specs=[vmem()] * 2,
        out_shape=[shape((rows, wide), f32), shape((rows, wide), bf16)],
        scratch_shapes=[pltpu.VMEM(kept.shape, f32)],
        compiler_params=params(8),
        cost_estimate=cost(2000),
    )(kept, got)


def scatter_kernel(kept, got, out):
    value = kept[...] + got[...].astype(f32)
    parts, rows = out.shape[0], out.shape[1]
    for p in range(parts):
        out[p] = value[p * rows : (p + 1) * rows].astype(out.dtype)


def ring(count, distance):
    return [(i, (i + distance) % count) for i in range(count)]


def local(latents, edge_weight, block_ids, block_count, w_in, w_out, targets, area, var_weight):
    members = latents.shape[1]
    feature = latents.shape[3]
    hidden = w_in.shape[0]
    variables = w_out.shape[0]
    rows_v = (variables + 7) // 8 * 8
    tiles, slots, cells, nodes = edge_weight.shape
    n = tiles * cells
    lat = latents[0].reshape(members, -1, nodes, feature)
    blocks = lat.shape[1]
    edge_rows = HALO * nodes
    rim_rows = 2 * edge_rows
    spaces = lax.axis_size("space")
    chips = lax.axis_size("member")
    ids = block_ids.T
    first = [(i, (((i + 1) ^ 1) - 1) % spaces) for i in range(spaces)]
    second = [(i, i ^ 1) for i in range(spaces)]

    edges = pl.pallas_call(
        edges_kernel,
        in_specs=[hbm()],
        out_specs=[vmem()] * 4,
        out_shape=[shape((edge_rows, feature), bf16)] * 4,
        scratch_shapes=[pltpu.SemaphoreType.DMA((4,))],
        compiler_params=params(8),
    )(in_hbm(latents[0]))
    halos = []
    for m in range(members):
        far = lax.ppermute(edges[2 * m + 1], "space", second)
        near = lax.ppermute(edges[2 * m], "space", first)
        halos.append((near, far))

    scale_n = area[None, :]

    acc0, acc1, halo_w, w_in_v, w_out_v, weight_v = pl.pallas_call(
        functools.partial(prepare_kernel, spaces=spaces),
        in_specs=[hbm()] * 5 + [vmem()],
        out_specs=[vmem()] * 6,
        out_shape=[
            held((n, feature), f32),
            held((n, feature), f32),
            held((n, rim_rows + nodes), bf16),
            held((hidden, feature), bf16),
            held((rows_v, hidden), bf16),
            held(edge_weight.shape, bf16),
        ],
        scratch_shapes=[
            pltpu.SMEM(ids.shape, jnp.int32),
            pltpu.SMEM(block_count.shape, jnp.int32),
            pltpu.VMEM(lat.shape, bf16),
            pltpu.SemaphoreType.DMA((6,)),
        ],
        compiler_params=params(12),
        cost_estimate=cost(2000),
    )(
        in_hbm(ids), in_hbm(block_count), in_hbm(lat), in_hbm(edge_weight), in_hbm(w_in),
        in_hbm(w_out),
    )

    def along(x, distance):
        return lax.ppermute(x, "member", ring(chips, distance))

    def fields_of(acc, near, far):
        return pl.pallas_call(
            fields_kernel,
            in_specs=[vmem()] * 6,
            out_specs=[vmem()] * 2,
            out_shape=[held((n, feature), bf16), shape((rows_v, n), bf16)],
            compiler_params=params(8),
            cost_estimate=cost(100),
        )(*in_vmem(acc), near, far, *in_vmem(halo_w, w_in_v, w_out_v))

    def slopes_of(lat_m):
        return pl.pallas_call(
            slopes_kernel,
            in_specs=[vmem()] * 2,
            out_specs=[vmem()] * 2,
            out_shape=[held((hidden, n), bf16)] * 2,
            compiler_params=params(8),
            cost_estimate=cost(100),
        )(*in_vmem(lat_m, w_in_v))

    lat0, fields0 = fields_of(acc0, *halos[0])
    left0 = along(fields0, 1)
    right0 = along(fields0, -1)
    lat1, fields1 = fields_of(acc1, *halos[1])
    right1 = along(fields1, -1)
    left1 = along(fields1, 1)
    fields = [fields0, fields1]
    first_lat, left0, right0 = lax.optimization_barrier((lat0, left0, right0))
    act0, slope0 = slopes_of(first_lat)
    far0 = along(left0, 1)
    second_lat, _ = lax.optimization_barrier((lat1, slope0))
    act1, slope1 = slopes_of(second_lat)
    held_right1, _ = lax.optimization_barrier((right1, slope0))
    far1 = along(held_right1, -1)
    grid_latent, acts, slopes = [lat0, lat1], [act0, act1], [slope0, slope1]

    own_rows = blocks * nodes
    turned, w_in_t, w_out_t, target, scale_v = pl.pallas_call(
        functools.partial(turn_kernel, spaces=spaces, blocks=blocks),
        in_specs=[smem(), smem()] + [vmem()] * 5 + [anywhere()],
        out_specs=[vmem()] * 5,
        out_shape=[
            held((own_rows + rim_rows + nodes, n), bf16),
            held((feature, hidden), bf16),
            held((hidden, rows_v), bf16),
            held((rows_v, n), bf16),
            held((rows_v, 1), f32),
        ],
        scratch_shapes=[pltpu.VMEM((128, 128), f32)],
        compiler_params=params(8),
        cost_estimate=cost(100),
    )(
        ids, block_count, *in_vmem(weight_v, w_in_v, w_out_v), targets[0], var_weight[None],
        slopes[1],
    )

    part0, part1 = pl.pallas_call(
        functools.partial(spread_kernel, ensemble=members * chips),
        in_specs=[vmem()] * 8,
        out_specs=[vmem()] * 2,
        out_shape=[held((rows_v, n), f32)] * 2,
        compiler_params=params(8),
        cost_estimate=cost(100),
    )(*fields, left0, left1, right0, right1, far0, *in_vmem(target))

    wide = feature + 128
    half_rows = hidden // 2
    grad_pre0, grad_pre1, keep, send = pl.pallas_call(
        functools.partial(
            weights_kernel,
            ensemble=members * chips,
            states=targets.shape[0] * lax.axis_size("dp"),
        ),
        in_specs=[vmem()] * 14,
        out_specs=[vmem()] * 4,
        out_shape=[
            held((hidden, n), bf16),
            held((hidden, n), bf16),
            shape((half_rows, wide), f32),
            shape((half_rows, wide), bf16),
        ],
        scratch_shapes=[pltpu.VMEM((hidden, feature), f32), pltpu.VMEM((hidden, 128), f32)],
        compiler_params=params(12),
        cost_estimate=cost(2000),
    )(
        *fields, far1, *in_vmem(part0, part1), scale_n, *in_vmem(scale_v),
        *in_vmem(*acts, *slopes, *grid_latent, w_out_t),
    )

    swapped = lax.ppermute(send, "dp", [(0, 1), (1, 0)])

    grad_grid0, grad_grid1, rim_near, rim_far = pl.pallas_call(
        functools.partial(rim_kernel, own_rows=own_rows),
        in_specs=[vmem()] * 4,
        out_specs=[vmem()] * 4,
        out_shape=[held((feature, n), bf16)] * 2 + [shape((members, edge_rows, feature), bf16)] * 2,
        compiler_params=params(8),
        cost_estimate=cost(2000),
    )(*in_vmem(grad_pre0, grad_pre1, turned, w_in_t))

    quarter = half_rows // chips
    pieces = 3
    size = (own_rows - 2 * edge_rows) // pieces

    def owned_of(member, grad_grid, base):
        whole = shape((members, blocks * nodes, feature), f32)
        aliased = {} if base is None else {2: 0}
        base = grad_grid if base is None else base
        return pl.pallas_call(
            functools.partial(owned_kernel, member=member, own_rows=own_rows),
            in_specs=[vmem()] * 2 + [anywhere()],
            out_specs=[hbm(), vmem()],
            out_shape=[whole, held((2, edge_rows, feature), f32)],
            scratch_shapes=[
                pltpu.VMEM((pieces, size, feature), f32),
                pltpu.SemaphoreType.DMA((pieces,)),
            ],
            input_output_aliases=aliased,
            compiler_params=params(8),
            cost_estimate=cost(2000),
        )(*in_vmem(grad_grid, turned), base)

    swapped, _ = lax.optimization_barrier((swapped, grad_grid0))
    kept, send = halve(keep, swapped, 2)
    got = lax.ppermute(send, "member", [(i, chips - 1 - i) for i in range(chips)])
    rim_near, rim_far, grad_grid0, _ = lax.optimization_barrier(
        (rim_near, rim_far, grad_grid0, send)
    )
    got_far = lax.ppermute(rim_far, "space", second)
    got_near = lax.ppermute(rim_near, "space", first)
    owned, edge0 = owned_of(0, grad_grid0, None)
    got, _ = lax.optimization_barrier((got, edge0))
    kept, send = halve(kept, got, 1)
    got = lax.ppermute(send, "member", [(i, i ^ 1) for i in range(chips)])
    grad_grid1, _ = lax.optimization_barrier((grad_grid1, send))
    owned, edge1 = owned_of(1, grad_grid1, owned)
    got, _ = lax.optimization_barrier((got, edge1))

    last_rows = quarter // spaces
    spread = pl.pallas_call(
        scatter_kernel,
        in_specs=[vmem()] * 2,
        out_specs=vmem(),
        out_shape=shape((spaces, last_rows, wide), bf16),
        compiler_params=params(8),
    )(kept, got)
    spread = lax.all_to_all(spread, "space", 0, 0, tiled=True)
    grad_latent, grad_w_in, grad_w_out = pl.pallas_call(
        finish_kernel,
        in_specs=[hbm()] + [vmem()] * 5,
        out_specs=[hbm(), vmem(), vmem()],
        out_shape=[
            shape(owned.shape, f32),
            shape((last_rows, feature), f32),
            shape((last_rows, variables), f32),
        ],
        scratch_shapes=[
            pltpu.VMEM((2 * members, edge_rows, feature), f32),
            pltpu.SemaphoreType.DMA((2 * members,)),
        ],
        input_output_aliases={0: 0},
        compiler_params=params(8),
    )(owned, *in_vmem(edge0, edge1), got_far, got_near, spread)
    return grad_latent[None], grad_w_in, grad_w_out.T


def solution(mesh):
    placed = (
        P("dp", "member", "space", None),
        P("space", None, None, None),
        P("space", None),
        P("space"),
        P(),
        P(),
        P("dp", None, "space"),
        P("space"),
        P(),
    )
    return jax.shard_map(
        local,
        mesh=mesh,
        in_specs=placed,
        out_specs=(
            P("dp", "member", "space", None),
            P(("dp", "member", "space"), None),
            P(None, ("dp", "member", "space")),
        ),
        check_vma=False,
    )
```

```python
import functools

import jax
import jax.numpy as jnp
from jax import lax
from jax.experimental import pallas as pl
from jax.experimental.pallas import tpu as pltpu
from jax.sharding import PartitionSpec as P

HALO = 2
smooth_square = 0.1 * 0.1
gelu_scale = 0.7978845608028654
gelu_cubic = 0.044715
MIB = 1 << 20
f32 = jnp.float32
bf16 = jnp.bfloat16

NN = (((1,), (0,)), ((), ()))
NT = (((1,), (1,)), ((), ()))


def dot(a, b, dims=NN):
    return lax.dot_general(a, b, dims, preferred_element_type=f32)


def vmem():
    return pl.BlockSpec(memory_space=pltpu.VMEM)


def smem():
    return pl.BlockSpec(memory_space=pltpu.SMEM)


def hbm():
    return pl.BlockSpec(memory_space=pltpu.HBM)


def in_hbm(x):
    return pltpu.with_memory_space_constraint(x, pltpu.HBM)


def in_vmem(*xs):
    return [pltpu.with_memory_space_constraint(x, pltpu.VMEM) for x in xs]


def held(dims, dtype):
    return pltpu.VMEM(dims, dtype)


def anywhere():
    return pl.BlockSpec(memory_space=pl.ANY)


def cost(mega):
    return pl.CostEstimate(flops=mega * 1_000_000, bytes_accessed=mega * 4000, transcendentals=0)


def params(mib):
    return pltpu.CompilerParams(vmem_limit_bytes=mib * MIB)


def shape(dims, dtype):
    return jax.ShapeDtypeStruct(dims, dtype)


def rows_at(start, size):
    return pl.ds(pl.multiple_of(start * size, size), size)


def parity():
    return lax.rem(lax.axis_index("space") + 1, 2)


def edges_kernel(lat, near0, far0, near1, far1, sems):
    step = near0.shape[0]
    last = lat.shape[1] - step
    odd = parity()
    top = pl.multiple_of((1 - odd) * last, step)
    bottom = pl.multiple_of(odd * last, step)
    copies = []
    for m, (near, far) in enumerate(((near0, far0), (near1, far1))):
        for out, start in ((near, top), (far, bottom)):
            copies.append(
                pltpu.make_async_copy(lat.at[m, pl.ds(start, step)], out, sems.at[len(copies)])
            )
            copies[-1].start()
    for copy in copies:
        copy.wait()


def halo_slot(e, blocks, spaces):
    at_space = lax.axis_index("space")
    odd = parity()
    below, above = e < HALO, e >= HALO + blocks
    outside = (below & (at_space > 0)) | (above & (at_space < spaces - 1))
    slot = jnp.where(below, e + (1 - odd) * HALO, e - HALO - blocks + odd * HALO)
    return outside, jnp.where(below | above, slot, 0)


def prepare_kernel(
    ids_hbm, count_hbm, lat_hbm, weight_hbm, w_in_hbm, w_out,
    acc0, acc1, halo_w, w_in_v, w_out_v, weight, ids, count, lat, sems, *, spaces,
):
    tiles, slots, cells, nodes = weight.shape
    blocks = lat.shape[1]
    copies = [
        pltpu.make_async_copy(ids_hbm, ids, sems.at[4]),
        pltpu.make_async_copy(count_hbm, count, sems.at[5]),
        pltpu.make_async_copy(weight_hbm, weight, sems.at[0]),
        pltpu.make_async_copy(lat_hbm.at[0], lat.at[0], sems.at[1]),
        pltpu.make_async_copy(lat_hbm.at[1], lat.at[1], sems.at[2]),
        pltpu.make_async_copy(w_in_hbm, w_in_v, sems.at[3]),
    ]
    for c in copies:
        c.start()
    halo_w[...] = jnp.zeros_like(halo_w)
    w_out_v[...] = jnp.zeros_like(w_out_v)
    w_out_v[: w_out.shape[0]] = w_out[...]
    for c in copies[:3]:
        c.wait()

    unused = halo_w.shape[1] // nodes - 1
    for t in range(tiles):
        rows = slice(t * cells, (t + 1) * cells)
        for k in range(slots):
            outside, slot = halo_slot(ids[k, t], blocks, spaces)
            slot = jnp.where((k < count[t]) & outside, slot, unused)
            halo_w[rows, rows_at(slot, nodes)] += weight[t, k]

    for m, acc in enumerate((acc0, acc1)):
        copies[3 + m].wait()
        for t in range(tiles):
            parts, at = [], []
            for k in range(slots):
                e = ids[k, t]
                mine = (k < count[t]) & (e >= HALO) & (e < HALO + blocks)
                w = weight[t, k]
                parts.append(jnp.where(mine, w, jnp.zeros_like(w)))
                at.append(jnp.clip(e - HALO, 0, blocks - 1))
            lhs = jnp.concatenate(parts, axis=1)
            rhs = jnp.concatenate([lat[m, a] for a in at], axis=0)
            acc[t * cells : (t + 1) * cells] = dot(lhs, rhs)
    copies[5].wait()


def turn_kernel(
    ids, count, weight, w_in, w_out, target, var_weight, later,
    turned, w_in_t, w_out_t, target_v, scale_v, square, *, spaces, blocks,
):
    tiles, slots, cells, nodes = weight.shape
    turned[...] = jnp.zeros_like(turned)
    w_in_t[...] = w_in[...].T
    w_out_t[...] = w_out[...].T
    variables = target.shape[0]
    target_v[...] = jnp.zeros_like(target_v)
    target_v[:variables] = target[...]
    square[...] = jnp.zeros_like(square)
    square[:1, :variables] = var_weight[...]
    scale_v[...] = square[...].T[: scale_v.shape[0], :1]
    unused = turned.shape[0] // nodes - 1
    for t in range(tiles):
        columns = slice(t * cells, (t + 1) * cells)
        for k in range(slots):
            e = ids[k, t]
            outside, slot = halo_slot(e, blocks, spaces)
            mine = (e >= HALO) & (e < HALO + blocks)
            block = jnp.where(mine, e - HALO, jnp.where(outside, blocks + slot, unused))
            block = jnp.where(k < count[t], block, unused)
            turned[rows_at(block, nodes), columns] += weight[t, k].T


def gelu_parts(x):
    square = x * x
    half = 0.5 + 0.5 * jnp.tanh(x * (gelu_scale + (gelu_scale * gelu_cubic) * square))
    return square, half


CHUNK = 256


def fields_kernel(acc, near, far, halo_w, w_in, w_out, lat_out, fields):
    count = acc.shape[0]
    half_k = near.shape[0]
    for start in range(0, count, 4 * CHUNK):
        at = slice(start, start + 4 * CHUNK)
        total = acc[at] + dot(halo_w[at, :half_k], near[...])
        total = total + dot(halo_w[at, half_k : 2 * half_k], far[...])
        rounded = total.astype(bf16)
        lat_out[at] = rounded
        pre = dot(w_in[...], rounded, NT)
        inner = pre * (gelu_scale + (gelu_scale * gelu_cubic) * (pre * pre))
        half = 0.5 + 0.5 * jnp.tanh(inner.astype(bf16))
        fields[:, at] = dot(w_out[...], pre.astype(bf16) * half).astype(bf16)


def slopes_kernel(lat, w_in, act_t, slope_t):
    count = lat.shape[0]
    for start in range(0, count, CHUNK):
        at = slice(start, start + CHUNK)
        x = dot(w_in[...], lat[at], NT)
        square, half = gelu_parts(x)
        act_t[:, at] = (x * half).astype(bf16)
        inner = x * (2.0 * gelu_scale + (6.0 * gelu_scale * gelu_cubic) * square)
        slope_t[:, at] = (half + half * (1.0 - half) * inner).astype(bf16)


def smooth_sign(u):
    return u * lax.rsqrt(u * u + smooth_square)


def spread_kernel(
    own0, own1, o10, o11, o20, o21, far0, target, part0, part1, *, ensemble,
):
    count = own0.shape[1]
    for start in range(0, count, CHUNK):
        at = slice(start, start + CHUNK)
        truth = target[:, at].astype(f32)
        mine = [own0[:, at].astype(f32), own1[:, at].astype(f32)]
        pair = smooth_sign(mine[0] - mine[1])
        spread = [pair, -pair]
        for other in (o10, o11, o20, o21, far0):
            theirs = other[:, at].astype(f32)
            for a in range(2):
                spread[a] = spread[a] + smooth_sign(mine[a] - theirs)
        for a, part in enumerate((part0, part1)):
            value = smooth_sign(mine[a] - truth) * (1.0 / ensemble)
            part[:, at] = value - spread[a] * (1.0 / (ensemble * (ensemble - 1)))


def weights_kernel(
    own0, own1, far1, part0, part1, area, var_weight,
    act0, act1, slope0, slope1, lat0, lat1, w_out_t,
    grad_pre0, grad_pre1, keep, send, total_in, total_out, *, ensemble, states,
):
    count = own0.shape[1]
    for start in range(0, count, CHUNK):
        at = slice(start, start + CHUNK)
        mine = [own0[:, at].astype(f32), own1[:, at].astype(f32)]
        theirs = far1[:, at].astype(f32)
        cell_weight = area[:, at] * var_weight[...] * (1.0 / states)
        cots = []
        for a, part in enumerate((part0, part1)):
            spread = smooth_sign(mine[a] - theirs)
            value = part[:, at] - spread * (1.0 / (ensemble * (ensemble - 1)))
            cots.append((cell_weight * value).astype(bf16))
        cot = jnp.concatenate(cots, axis=1)
        grad_act = dot(w_out_t[...], cot)
        slope = jnp.concatenate([slope0[:, at], slope1[:, at]], axis=1)
        pre = (grad_act * slope.astype(f32)).astype(bf16)
        grad_pre0[:, at] = pre[:, :CHUNK]
        grad_pre1[:, at] = pre[:, CHUNK:]
        part_in = dot(pre, jnp.concatenate([lat0[at], lat1[at]], axis=0))
        act = jnp.concatenate([act0[:, at], act1[:, at]], axis=1)
        part_out = dot(act, cot, NT)
        if start == 0:
            total_in[...] = part_in
            total_out[...] = jnp.zeros_like(total_out)
            total_out[:, : part_out.shape[1]] = part_out
        else:
            total_in[...] += part_in
            total_out[:, : part_out.shape[1]] += part_out
    rows = keep.shape[0]
    wide = total_in.shape[1]
    here = lax.axis_index("dp")
    stay, leave = rows_at(here, rows), rows_at(1 - here, rows)
    keep[:, :wide] = total_in[stay]
    keep[:, wide:] = total_out[stay]
    send[:, :wide] = total_in[leave].astype(bf16)
    send[:, wide:] = total_out[leave].astype(bf16)


def rim_kernel(
    grad_pre0, grad_pre1, turned, w_in_t, grad_grid0, grad_grid1, near, far, *, own_rows,
):
    half_k = near.shape[1]
    for m, (grad_pre, grad_grid) in enumerate(
        ((grad_pre0, grad_grid0), (grad_pre1, grad_grid1))
    ):
        grad_grid[...] = dot(w_in_t[...], grad_pre[...]).astype(bf16)
        rims = dot(turned[own_rows : own_rows + 2 * half_k], grad_grid[...], NT).astype(bf16)
        near[m] = rims[:half_k]
        far[m] = rims[half_k:]


def owned_kernel(grad_grid, turned, base, out, edge, parts, sems, *, member, own_rows):
    step, size = edge.shape[1], parts.shape[1]
    copies = []
    for slot in range(parts.shape[0]):
        start = step + slot * size
        parts[slot] = dot(turned[start : start + size], grad_grid[...], NT)
        copy = pltpu.make_async_copy(
            parts.at[slot], out.at[member, start : start + size], sems.at[slot]
        )
        copy.start()
        copies.append(copy)
    ends = jnp.concatenate([turned[:step], turned[own_rows - step : own_rows]], axis=0)
    value = dot(ends, grad_grid[...], NT)
    edge[0] = value[:step]
    edge[1] = value[step:]
    for copy in copies:
        copy.wait()


def finish_kernel(
    base, edge0, edge1, far, near, got, out, grad_in, grad_out, parts, sems,
):
    step = edge0.shape[1]
    last = out.shape[1] - step
    odd = parity()
    copies = []
    for side, rim in ((1 - odd, near), (odd, far)):
        start = pl.multiple_of(side * last, step)
        for m, edge in enumerate((edge0, edge1)):
            slot = len(copies)
            parts[slot] = edge[side] + rim[m].astype(f32)
            copy = pltpu.make_async_copy(
                parts.at[slot], out.at[m, pl.ds(start, step)], sems.at[slot]
            )
            copy.start()
            copies.append(copy)
    value = got[0].astype(f32)
    for p in range(1, got.shape[0]):
        value = value + got[p].astype(f32)
    wide = grad_in.shape[1]
    grad_in[...] = value[:, :wide]
    grad_out[...] = value[:, wide : wide + grad_out.shape[1]]
    for copy in copies:
        copy.wait()


def halve_kernel(kept, got, keep, send, total, *, bit):
    rows = keep.shape[0]
    total[...] = kept[...] + got[...].astype(f32)
    here = lax.rem(lax.axis_index("member") // bit, 2)
    keep[...] = total[rows_at(here, rows)]
    send[...] = total[rows_at(1 - here, rows)].astype(send.dtype)


def halve(kept, got, bit):
    rows, wide = kept.shape[0] // 2, kept.shape[1]
    return pl.pallas_call(
        functools.partial(halve_kernel, bit=bit),
        in_specs=[vmem()] * 2,
        out_specs=[vmem()] * 2,
        out_shape=[shape((rows, wide), f32), shape((rows, wide), bf16)],
        scratch_shapes=[pltpu.VMEM(kept.shape, f32)],
        compiler_params=params(8),
        cost_estimate=cost(2000),
    )(kept, got)


def scatter_kernel(kept, got, out):
    value = kept[...] + got[...].astype(f32)
    parts, rows = out.shape[0], out.shape[1]
    for p in range(parts):
        out[p] = value[p * rows : (p + 1) * rows].astype(out.dtype)


def ring(count, distance):
    return [(i, (i + distance) % count) for i in range(count)]


def local(latents, edge_weight, block_ids, block_count, w_in, w_out, targets, area, var_weight):
    members = latents.shape[1]
    feature = latents.shape[3]
    hidden = w_in.shape[0]
    variables = w_out.shape[0]
    rows_v = (variables + 7) // 8 * 8
    tiles, slots, cells, nodes = edge_weight.shape
    n = tiles * cells
    lat = latents[0].reshape(members, -1, nodes, feature)
    blocks = lat.shape[1]
    edge_rows = HALO * nodes
    rim_rows = 2 * edge_rows
    spaces = lax.axis_size("space")
    chips = lax.axis_size("member")
    ids = block_ids.T
    first = [(i, (((i + 1) ^ 1) - 1) % spaces) for i in range(spaces)]
    second = [(i, i ^ 1) for i in range(spaces)]

    edges = pl.pallas_call(
        edges_kernel,
        in_specs=[hbm()],
        out_specs=[vmem()] * 4,
        out_shape=[shape((edge_rows, feature), bf16)] * 4,
        scratch_shapes=[pltpu.SemaphoreType.DMA((4,))],
        compiler_params=params(8),
    )(in_hbm(latents[0]))
    halos = []
    for m in range(members):
        far = lax.ppermute(edges[2 * m + 1], "space", second)
        near = lax.ppermute(edges[2 * m], "space", first)
        halos.append((near, far))

    scale_n = area[None, :]

    acc0, acc1, halo_w, w_in_v, w_out_v, weight_v = pl.pallas_call(
        functools.partial(prepare_kernel, spaces=spaces),
        in_specs=[hbm()] * 5 + [vmem()],
        out_specs=[vmem()] * 6,
        out_shape=[
            held((n, feature), f32),
            held((n, feature), f32),
            held((n, rim_rows + nodes), bf16),
            held((hidden, feature), bf16),
            held((rows_v, hidden), bf16),
            held(edge_weight.shape, bf16),
        ],
        scratch_shapes=[
            pltpu.SMEM(ids.shape, jnp.int32),
            pltpu.SMEM(block_count.shape, jnp.int32),
            pltpu.VMEM(lat.shape, bf16),
            pltpu.SemaphoreType.DMA((6,)),
        ],
        compiler_params=params(12),
        cost_estimate=cost(2000),
    )(
        in_hbm(ids), in_hbm(block_count), in_hbm(lat), in_hbm(edge_weight), in_hbm(w_in),
        in_hbm(w_out),
    )

    def along(x, distance):
        return lax.ppermute(x, "member", ring(chips, distance))

    def fields_of(acc, near, far):
        return pl.pallas_call(
            fields_kernel,
            in_specs=[vmem()] * 6,
            out_specs=[vmem()] * 2,
            out_shape=[held((n, feature), bf16), shape((rows_v, n), bf16)],
            compiler_params=params(8),
            cost_estimate=cost(100),
        )(*in_vmem(acc), near, far, *in_vmem(halo_w, w_in_v, w_out_v))

    def slopes_of(lat_m):
        return pl.pallas_call(
            slopes_kernel,
            in_specs=[vmem()] * 2,
            out_specs=[vmem()] * 2,
            out_shape=[held((hidden, n), bf16)] * 2,
            compiler_params=params(8),
            cost_estimate=cost(100),
        )(*in_vmem(lat_m, w_in_v))

    lat0, fields0 = fields_of(acc0, *halos[0])
    left0 = along(fields0, 1)
    right0 = along(fields0, -1)
    lat1, fields1 = fields_of(acc1, *halos[1])
    right1 = along(fields1, -1)
    left1 = along(fields1, 1)
    fields = [fields0, fields1]
    first_lat, left0, right0 = lax.optimization_barrier((lat0, left0, right0))
    act0, slope0 = slopes_of(first_lat)
    far0 = along(left0, 1)
    second_lat, _ = lax.optimization_barrier((lat1, slope0))
    act1, slope1 = slopes_of(second_lat)
    held_right1, _ = lax.optimization_barrier((right1, slope0))
    far1 = along(held_right1, -1)
    grid_latent, acts, slopes = [lat0, lat1], [act0, act1], [slope0, slope1]

    own_rows = blocks * nodes
    turned, w_in_t, w_out_t, target, scale_v = pl.pallas_call(
        functools.partial(turn_kernel, spaces=spaces, blocks=blocks),
        in_specs=[smem(), smem()] + [vmem()] * 5 + [anywhere()],
        out_specs=[vmem()] * 5,
        out_shape=[
            held((own_rows + rim_rows + nodes, n), bf16),
            held((feature, hidden), bf16),
            held((hidden, rows_v), bf16),
            held((rows_v, n), bf16),
            held((rows_v, 1), f32),
        ],
        scratch_shapes=[pltpu.VMEM((128, 128), f32)],
        compiler_params=params(8),
        cost_estimate=cost(100),
    )(
        ids, block_count, *in_vmem(weight_v, w_in_v, w_out_v), targets[0], var_weight[None],
        slopes[1],
    )

    part0, part1 = pl.pallas_call(
        functools.partial(spread_kernel, ensemble=members * chips),
        in_specs=[vmem()] * 8,
        out_specs=[vmem()] * 2,
        out_shape=[held((rows_v, n), f32)] * 2,
        compiler_params=params(8),
        cost_estimate=cost(100),
    )(*fields, left0, left1, right0, right1, far0, *in_vmem(target))

    wide = feature + 128
    half_rows = hidden // 2
    grad_pre0, grad_pre1, keep, send = pl.pallas_call(
        functools.partial(
            weights_kernel,
            ensemble=members * chips,
            states=targets.shape[0] * lax.axis_size("dp"),
        ),
        in_specs=[vmem()] * 14,
        out_specs=[vmem()] * 4,
        out_shape=[
            held((hidden, n), bf16),
            held((hidden, n), bf16),
            shape((half_rows, wide), f32),
            shape((half_rows, wide), bf16),
        ],
        scratch_shapes=[pltpu.VMEM((hidden, feature), f32), pltpu.VMEM((hidden, 128), f32)],
        compiler_params=params(12),
        cost_estimate=cost(2000),
    )(
        *fields, far1, *in_vmem(part0, part1), scale_n, *in_vmem(scale_v),
        *in_vmem(*acts, *slopes, *grid_latent, w_out_t),
    )

    swapped = lax.ppermute(send, "dp", [(0, 1), (1, 0)])

    grad_grid0, grad_grid1, rim_near, rim_far = pl.pallas_call(
        functools.partial(rim_kernel, own_rows=own_rows),
        in_specs=[vmem()] * 4,
        out_specs=[vmem()] * 4,
        out_shape=[held((feature, n), bf16)] * 2 + [shape((members, edge_rows, feature), bf16)] * 2,
        compiler_params=params(8),
        cost_estimate=cost(2000),
    )(*in_vmem(grad_pre0, grad_pre1, turned, w_in_t))

    quarter = half_rows // chips
    pieces = 3
    size = (own_rows - 2 * edge_rows) // pieces

    def owned_of(member, grad_grid, base):
        whole = shape((members, blocks * nodes, feature), f32)
        aliased = {} if base is None else {2: 0}
        base = grad_grid if base is None else base
        return pl.pallas_call(
            functools.partial(owned_kernel, member=member, own_rows=own_rows),
            in_specs=[vmem()] * 2 + [anywhere()],
            out_specs=[hbm(), vmem()],
            out_shape=[whole, held((2, edge_rows, feature), f32)],
            scratch_shapes=[
                pltpu.VMEM((pieces, size, feature), f32),
                pltpu.SemaphoreType.DMA((pieces,)),
            ],
            input_output_aliases=aliased,
            compiler_params=params(8),
            cost_estimate=cost(2000),
        )(*in_vmem(grad_grid, turned), base)

    swapped, _ = lax.optimization_barrier((swapped, grad_grid0))
    kept, send = halve(keep, swapped, 2)
    got = lax.ppermute(send, "member", [(i, chips - 1 - i) for i in range(chips)])
    rim_near, rim_far, grad_grid0, _ = lax.optimization_barrier(
        (rim_near, rim_far, grad_grid0, send)
    )
    got_far = lax.ppermute(rim_far, "space", second)
    got_near = lax.ppermute(rim_near, "space", first)
    owned, edge0 = owned_of(0, grad_grid0, None)
    got, _ = lax.optimization_barrier((got, edge0))
    kept, send = halve(kept, got, 1)
    got = lax.ppermute(send, "member", [(i, i ^ 1) for i in range(chips)])
    grad_grid1, _ = lax.optimization_barrier((grad_grid1, send))
    owned, edge1 = owned_of(1, grad_grid1, owned)
    got, _ = lax.optimization_barrier((got, edge1))

    last_rows = quarter // spaces
    spread = pl.pallas_call(
        scatter_kernel,
        in_specs=[vmem()] * 2,
        out_specs=vmem(),
        out_shape=shape((spaces, last_rows, wide), bf16),
        compiler_params=params(8),
    )(kept, got)
    spread = lax.all_to_all(spread, "space", 0, 0, tiled=True)
    grad_latent, grad_w_in, grad_w_out = pl.pallas_call(
        finish_kernel,
        in_specs=[hbm()] + [vmem()] * 5,
        out_specs=[hbm(), vmem(), vmem()],
        out_shape=[
            shape(owned.shape, f32),
            shape((last_rows, feature), f32),
            shape((last_rows, variables), f32),
        ],
        scratch_shapes=[
            pltpu.VMEM((2 * members, edge_rows, feature), f32),
            pltpu.SemaphoreType.DMA((2 * members,)),
        ],
        input_output_aliases={0: 0},
        compiler_params=params(8),
    )(owned, *in_vmem(edge0, edge1), got_far, got_near, spread)
    return grad_latent[None], grad_w_in, grad_w_out.T


def solution(mesh):
    placed = (
        P("dp", "member", "space", None),
        P("space", None, None, None),
        P("space", None),
        P("space"),
        P(),
        P(),
        P("dp", None, "space"),
        P("space"),
        P(),
    )
    return jax.shard_map(
        local,
        mesh=mesh,
        in_specs=placed,
        out_specs=(
            P("dp", "member", "space", None),
            P(("dp", "member", "space"), None),
            P(None, ("dp", "member", "space")),
        ),
        check_vma=False,
    )
```
